256 devices in a mesh: loop: 64 (over z, x, y_lo), grp: 4 (over y_hi, core).
Axes of the slice: x: 4, y: 4 (y_hi: 2, y_lo: 2; y = y_hi * 2 + y_lo), z: 8, core: 2. Of those that a mesh axis runs over, the one named last changes fastest.
Arguments:
- slab: bfloat16 [2048, 524288], P(None, ('loop', 'grp')), may hold values from -64 to 64
- sketch: bfloat16 [524288, 256], P(('loop', 'grp')), may hold values from -0.0078125 to 0.0078125
Outputs:
- basis: float32 [2048, 512], P(('loop', 'grp'))
The draws below stay inside these ranges and needn't reach their ends.
All inputs are finite; a program needn't handle non-finite values.
Results may differ from the reference program's by a relative error of at most 0.0003.
Values may be sent and summed in bfloat16 or wider, within the bound.
No kernel may reach another device: no remote copies, remote signals or barrier semaphores. Data moves between devices by JAX's collectives and lax.ppermute only.
A program may use at most 64 MiB of HBM per device.

```python
import math
import jax
import jax.numpy as jnp
from jax import lax

C_DEV = 2048
K = 256
ROWS = 2048
NCOL = 524288
N_LOOP = 64
N_GRP = 4


def draw_slab(key, part):
    key = jax.random.fold_in(key, 11)
    key_main, key_rows, key_cols = jax.random.split(key, 3)
    rise = jnp.exp(math.log(3.0) * jnp.arange(ROWS, dtype=jnp.float32) / ROWS)
    row_scale = jnp.exp(jax.random.uniform(key_rows, (ROWS, 1), jnp.float32) * math.log(10.0)) * rise[:, None]
    col_scale = jnp.exp(jax.random.uniform(key_cols, (1, NCOL), jnp.float32) * math.log(10.0)) / 4.6
    values = jax.random.normal(key_main, (ROWS, NCOL), jnp.float32)
    return jnp.clip(values * row_scale * col_scale, -64.0, 64.0).astype(jnp.bfloat16)


def shard_levels(key, dims, cuts, least, high):
    loudness = 1.0
    for axis_at, parts in cuts:
        draws = jax.random.uniform(jax.random.fold_in(jax.random.fold_in(key, 6), axis_at), (parts,), jnp.float32, least / len(cuts), high / len(cuts))
        loudness = loudness * jnp.repeat(jnp.exp(draws), dims[axis_at] // parts).reshape((-1,) + (1,) * (len(dims) - 1 - axis_at))
    return loudness


def normal_values(key, dims, scale, bound, pieces=(), kind=jnp.bfloat16):
    values = jax.random.normal(key, dims, jnp.float32) * scale
    if len(pieces) > 0:
        values = shard_levels(key, dims, pieces, -0.22, 0.18) * values
    return jnp.clip(values, min=-bound, max=bound).astype(kind)


def setup_inputs(seed: int = 0) -> dict:
    seeds = jax.random.split(jax.random.key(seed), 3)
    slab = draw_slab(jax.random.fold_in(seeds[2], 71), 0)
    sketch = normal_values(seeds[1], (NCOL, K), NCOL ** -0.5, 0.0078125, ((0, 256),))
    return dict(slab=slab, sketch=sketch)


def reference(slab, sketch):
    rotated = jnp.roll(sketch, C_DEV * N_GRP, axis=0)
    both = jnp.concatenate((sketch, rotated), axis=1)
    width = C_DEV * N_GRP

    def add_block(index, total):
        start = (index * width).astype(jnp.int32)
        columns = lax.dynamic_slice_in_dim(slab, start, width, 1)
        tiles = lax.dynamic_slice_in_dim(both, start, width, 0)
        return total + jnp.dot(columns.astype(jnp.float32), tiles.astype(jnp.float32), preferred_element_type=jnp.float32)
    projected = lax.fori_loop(0, N_LOOP, add_block, jnp.zeros((ROWS, 2 * K), jnp.float32))
    gram = jnp.dot(projected.T.astype(jnp.float32), projected.astype(jnp.float32), precision=lax.Precision.HIGHEST, preferred_element_type=jnp.float32)
    lower = jnp.linalg.cholesky(gram)
    solved = jax.scipy.linalg.solve_triangular(lower, projected.T, lower=True)
    return solved.T * math.sqrt(ROWS)
```

```python
import math

import jax
import jax.numpy as jnp
from jax import lax
from jax.sharding import Mesh, PartitionSpec as P

ROWS = 2048
PLANE = ("x", "yl", "yh")
DEVICE = ("z", "x", "yl", "yh", "c")


def shifted(block):
    loop = ("z", "x", "yl")
    size = lax.axis_size(loop)
    return lax.ppermute(block, loop, [(i, (i + 1) % size) for i in range(size)])


def core_swap(block):
    return lax.ppermute(block, "c", [(0, 1), (1, 0)])


def spread(block, axes):
    return lax.all_to_all(block, axes, 0, 0, tiled=True)


def gathered(block, axes):
    size = lax.axis_size(axes)
    return spread(jnp.broadcast_to(block[None], (size,) + block.shape), axes)


def scattered_sum(partial):
    depth, width = lax.axis_size("z"), lax.axis_size(PLANE)
    rows, cols = partial.shape
    unit = rows // (depth * width * 2)
    pieces = partial.reshape(depth, width, 2, unit, cols)
    core = lax.axis_index("c")
    away = lax.dynamic_index_in_dim(pieces, 1 - core, 2, keepdims=False)
    kept = lax.dynamic_index_in_dim(pieces, core, 2, keepdims=False)
    chip = (kept + core_swap(away)).transpose(1, 0, 2, 3)
    plane = spread(chip, PLANE).sum(axis=0)
    return spread(plane, "z").sum(axis=0)


def full_gram(own_rows):
    wide = PLANE + ("c",)
    count = lax.axis_size(wide)
    rows = gathered(own_rows, wide).reshape(-1, own_rows.shape[1])
    cols = rows.shape[1]
    unit = cols // count
    mine = lax.dynamic_slice_in_dim(rows, lax.axis_index(wide) * unit, unit, 1)
    part = lax.dot_general(
        mine,
        rows,
        (((0,), (0,)), ((), ())),
        precision=lax.Precision.HIGHEST,
        preferred_element_type=jnp.float32,
    )
    part = gathered(part, "z").sum(axis=0)
    return gathered(part, wide).reshape(cols, cols)


def body(slab, sketch):
    moved = shifted(sketch)
    own_part = jnp.dot(slab, sketch, preferred_element_type=jnp.float32)
    far_part = jnp.dot(slab, moved, preferred_element_type=jnp.float32)
    own_rows = scattered_sum(jnp.concatenate((own_part, far_part), axis=1))
    gram = full_gram(own_rows)
    lower = jnp.linalg.cholesky(gram)
    solved = jax.scipy.linalg.solve_triangular(lower, own_rows.T, lower=True)
    return solved.T * math.sqrt(ROWS)


def solution(mesh):
    fine = Mesh(mesh.devices.reshape(8, 4, 2, 2, 2), DEVICE)
    return jax.shard_map(
        body,
        mesh=fine,
        in_specs=(P(None, DEVICE), P(DEVICE, None)),
        out_specs=P(DEVICE, None),
        check_vma=False,
    )
```

```python
import functools
import math

import jax
import jax.numpy as jnp
from jax import lax
from jax.experimental import pallas as pl
from jax.experimental.pallas import tpu as pltpu
from jax.sharding import Mesh, PartitionSpec as P

ROWS = 2048
B = 128
HI = lax.Precision.HIGHEST
PLANE = ("x", "yl", "yh")
DEVICE = ("z", "x", "yl", "yh", "c")


def wide(row):
    return jnp.broadcast_to(row, (8, B))


def nt(a, b):
    return lax.dot_general(a, b, (((1,), (1,)), ((), ())), precision=HI, preferred_element_type=jnp.float32)


def eliminate(w_ref, c_ref, s):
    r0 = 8 * s
    top = w_ref[r0 : r0 + 8, :B]
    for j in range(8):
        c_ref[8 * j : 8 * j + 8, :] = wide(top[:, r0 + j : r0 + j + 1])
    schur = {(i, j): wide(c_ref[8 * j + i : 8 * j + i + 1, :]) for j in range(8) for i in range(j, 8)}
    rows = [[wide(w_ref[r0 + i : r0 + i + 1, t * B : (t + 1) * B]) for t in range(2)] for i in range(8)]
    ratio, inverse = {}, []
    for j in range(8):
        inv = 1.0 / schur[j, j]
        inverse.append(inv)
        for i in range(j + 1, 8):
            ratio[i, j] = schur[i, j] * inv
        for i in range(j + 1, 8):
            for k in range(j + 1, i + 1):
                schur[i, k] = schur[i, k] - ratio[i, j] * schur[k, j]
        for i in range(j + 1, 8):
            for t in range(2):
                rows[i][t] = rows[i][t] - ratio[i, j] * rows[j][t]
    for i in range(8):
        w_ref[r0 + i : r0 + i + 1, B:] = (rows[i][1] * lax.rsqrt(schur[i, i]))[:1]
    if s == B // 8 - 1:
        return
    g = [None] * 8
    for i in reversed(range(8)):
        g[i] = [rows[i][t] * inverse[i] for t in range(2)]
        for k in range(i + 1, 8):
            for t in range(2):
                g[i][t] = g[i][t] - ratio[k, i] * g[k][t]
    for v in range(s + 1, B // 8):
        at = slice(8 * v, 8 * v + 8)
        left, right = w_ref[at, :B], w_ref[at, B:]
        new_left, new_right = left, right
        for j in range(8):
            col = wide(left[:, r0 + j : r0 + j + 1])
            new_left = new_left - col * g[j][0]
            new_right = new_right - col * g[j][1]
        w_ref[at, :B] = new_left
        w_ref[at, B:] = new_right


def kernel(scale, gram_ref, rows_ref, out_ref, a_ref, w_ref, c_ref):
    n = gram_ref.shape[0]
    a_ref[:n] = gram_ref[...]
    a_ref[n:] = rows_ref[...]
    eye = (lax.broadcasted_iota(jnp.int32, (B, B), 0) == lax.broadcasted_iota(jnp.int32, (B, B), 1)).astype(jnp.float32)
    for k in range(n // B):
        lo, hi = k * B, (k + 1) * B
        w_ref[:, :B] = a_ref[lo:hi, lo:hi]
        w_ref[:, B:] = eye
        for s in range(B // 8):
            eliminate(w_ref, c_ref, s)
        inv = w_ref[:, B:]
        panel = nt(a_ref[hi:, lo:hi], inv)
        out_ref[:, lo:hi] = panel[n - hi :] * scale
        if hi < n:
            a_ref[hi:, hi:] = a_ref[hi:, hi:] - nt(panel, panel[: n - hi])


def solve_rows(gram, rows, scale):
    n = gram.shape[0]
    return pl.pallas_call(
        functools.partial(kernel, scale),
        out_shape=jax.ShapeDtypeStruct(rows.shape, jnp.float32),
        in_specs=[pl.BlockSpec(memory_space=pltpu.VMEM)] * 2,
        out_specs=pl.BlockSpec(memory_space=pltpu.VMEM),
        scratch_shapes=[
            pltpu.VMEM((n + 8, n), jnp.float32),
            pltpu.VMEM((B, 2 * B), jnp.float32),
            pltpu.VMEM((64, B), jnp.float32),
        ],
        compiler_params=pltpu.CompilerParams(vmem_limit_bytes=16 * 1024 * 1024),
    )(gram, rows)


def shifted(block):
    loop = ("z", "x", "yl")
    size = lax.axis_size(loop)
    return lax.ppermute(block, loop, [(i, (i + 1) % size) for i in range(size)])


def core_swap(block):
    return lax.ppermute(block, "c", [(0, 1), (1, 0)])


def spread(block, axes):
    return lax.all_to_all(block, axes, 0, 0, tiled=True)


def gathered(block, axes):
    size = lax.axis_size(axes)
    return spread(jnp.broadcast_to(block[None], (size,) + block.shape), axes)


def scattered_sum(partial):
    depth, width = lax.axis_size("z"), lax.axis_size(PLANE)
    rows, cols = partial.shape
    unit = rows // (depth * width * 2)
    pieces = partial.reshape(depth, width, 2, unit, cols)
    core = lax.axis_index("c")
    away = lax.dynamic_index_in_dim(pieces, 1 - core, 2, keepdims=False)
    kept = lax.dynamic_index_in_dim(pieces, core, 2, keepdims=False)
    chip = (kept + core_swap(away)).transpose(1, 0, 2, 3)
    plane = spread(chip, PLANE).sum(axis=0)
    return spread(plane, "z").sum(axis=0)


def full_gram(own_rows):
    wide = PLANE + ("c",)
    count = lax.axis_size(wide)
    rows = gathered(own_rows, wide).reshape(-1, own_rows.shape[1])
    cols = rows.shape[1]
    unit = cols // count
    mine = lax.dynamic_slice_in_dim(rows, lax.axis_index(wide) * unit, unit, 1)
    part = lax.dot_general(
        mine,
        rows,
        (((0,), (0,)), ((), ())),
        precision=HI,
        preferred_element_type=jnp.float32,
    )
    part = gathered(part, "z").sum(axis=0)
    return gathered(part, wide).reshape(cols, cols)


def body(slab, sketch):
    moved = shifted(sketch)
    own_part = jnp.dot(slab, sketch, preferred_element_type=jnp.float32)
    far_part = jnp.dot(slab, moved, preferred_element_type=jnp.float32)
    own_rows = scattered_sum(jnp.concatenate((own_part, far_part), axis=1))
    gram = full_gram(own_rows)
    return solve_rows(gram, own_rows, math.sqrt(ROWS))


def solution(mesh):
    fine = Mesh(mesh.devices.reshape(8, 4, 2, 2, 2), DEVICE)
    return jax.shard_map(
        body,
        mesh=fine,
        in_specs=(P(None, DEVICE), P(DEVICE, None)),
        out_specs=P(DEVICE, None),
        check_vma=False,
    )
```

```python
import functools
import math

import jax
import jax.numpy as jnp
from jax import lax
from jax.experimental import pallas as pl
from jax.experimental.pallas import tpu as pltpu
from jax.sharding import Mesh, PartitionSpec as P

ROWS = 2048
B = 128
HI = lax.Precision.HIGHEST
PLANE = ("x", "yl", "yh")
DEVICE = ("z", "x", "yl", "yh", "c")


def wide(row):
    return jnp.broadcast_to(row, (8, B))


def nt(a, b):
    return lax.dot_general(a, b, (((1,), (1,)), ((), ())), precision=HI, preferred_element_type=jnp.float32)


def eliminate(w_ref, c_ref, s):
    r0 = 8 * s
    top = w_ref[r0 : r0 + 8, :B]
    for j in range(8):
        c_ref[8 * j : 8 * j + 8, :] = wide(top[:, r0 + j : r0 + j + 1])
    schur = {(i, j): wide(c_ref[8 * j + i : 8 * j + i + 1, :]) for j in range(8) for i in range(j, 8)}
    rows = [[wide(w_ref[r0 + i : r0 + i + 1, t * B : (t + 1) * B]) for t in range(2)] for i in range(8)]
    ratio, inverse = {}, []
    for j in range(8):
        inv = 1.0 / schur[j, j]
        inverse.append(inv)
        for i in range(j + 1, 8):
            ratio[i, j] = schur[i, j] * inv
        for i in range(j + 1, 8):
            for k in range(j + 1, i + 1):
                schur[i, k] = schur[i, k] - ratio[i, j] * schur[k, j]
        for i in range(j + 1, 8):
            for t in range(2):
                rows[i][t] = rows[i][t] - ratio[i, j] * rows[j][t]
    for i in range(8):
        w_ref[r0 + i : r0 + i + 1, B:] = (rows[i][1] * lax.rsqrt(schur[i, i]))[:1]
    if s == B // 8 - 1:
        return
    g = [None] * 8
    for i in reversed(range(8)):
        g[i] = [rows[i][t] * inverse[i] for t in range(2)]
        for k in range(i + 1, 8):
            for t in range(2):
                g[i][t] = g[i][t] - ratio[k, i] * g[k][t]
    for v in range(s + 1, B // 8):
        at = slice(8 * v, 8 * v + 8)
        left, right = w_ref[at, :B], w_ref[at, B:]
        new_left, new_right = left, right
        for j in range(8):
            col = wide(left[:, r0 + j : r0 + j + 1])
            new_left = new_left - col * g[j][0]
            new_right = new_right - col * g[j][1]
        w_ref[at, :B] = new_left
        w_ref[at, B:] = new_right


def kernel(scale, gram_ref, rows_ref, out_ref, a_ref, w_ref, c_ref):
    n = gram_ref.shape[0]
    a_ref[:n] = gram_ref[...]
    a_ref[n:] = rows_ref[...]
    eye = (lax.broadcasted_iota(jnp.int32, (B, B), 0) == lax.broadcasted_iota(jnp.int32, (B, B), 1)).astype(jnp.float32)
    for k in range(n // B):
        lo, hi = k * B, (k + 1) * B
        w_ref[:, :B] = a_ref[lo:hi, lo:hi]
        w_ref[:, B:] = eye
        for s in range(B // 8):
            eliminate(w_ref, c_ref, s)
        inv = w_ref[:, B:]
        panel = nt(a_ref[hi:, lo:hi], inv)
        out_ref[:, lo:hi] = panel[n - hi :] * scale
        if hi < n:
            a_ref[hi:, hi:] = a_ref[hi:, hi:] - nt(panel, panel[: n - hi])


def solve_rows(gram, rows, scale):
    n = gram.shape[0]
    return pl.pallas_call(
        functools.partial(kernel, scale),
        out_shape=jax.ShapeDtypeStruct(rows.shape, jnp.float32),
        in_specs=[pl.BlockSpec(memory_space=pltpu.VMEM)] * 2,
        out_specs=pl.BlockSpec(memory_space=pltpu.VMEM),
        scratch_shapes=[
            pltpu.VMEM((n + 8, n), jnp.float32),
            pltpu.VMEM((B, 2 * B), jnp.float32),
            pltpu.VMEM((64, B), jnp.float32),
        ],
        compiler_params=pltpu.CompilerParams(vmem_limit_bytes=16 * 1024 * 1024),
    )(gram, rows)


def shifted(block):
    loop = ("z", "x", "yl")
    size = lax.axis_size(loop)
    return lax.ppermute(block, loop, [(i, (i + 1) % size) for i in range(size)])


def core_swap(block):
    return lax.ppermute(block, "c", [(0, 1), (1, 0)])


def spread(block, axes):
    return lax.all_to_all(block, axes, 0, 0, tiled=True)


def gathered(block, axes):
    size = lax.axis_size(axes)
    return spread(jnp.broadcast_to(block[None], (size,) + block.shape), axes)


def product_kernel(slab_ref, sketch_ref, after_ref, kept_ref, away_ref):
    width, unit, cols = kept_ref.shape[0], kept_ref.shape[2], kept_ref.shape[3]
    total = jnp.dot(slab_ref[...], sketch_ref[...], preferred_element_type=jnp.float32)
    pairs = total.reshape(width, 2, unit, cols)
    first = lax.axis_index("c") == 0
    kept_ref[:, 0] = jnp.where(first, pairs[:, 0], pairs[:, 1])
    away_ref[:, 0] = jnp.where(first, pairs[:, 1], pairs[:, 0])


def product(slab, sketch, after):
    depth, width = lax.axis_size("z"), lax.axis_size(PLANE)
    rows, inner = slab.shape
    cols = sketch.shape[1]
    unit = rows // (depth * width * 2)
    half = pl.BlockSpec((width, 1, unit, cols), lambda z: (0, z, 0, 0))
    shape = jax.ShapeDtypeStruct((width, depth, unit, cols), jnp.float32)
    return pl.pallas_call(
        product_kernel,
        grid=(depth,),
        in_specs=[pl.BlockSpec((rows // depth, inner), lambda z: (z, 0)), pl.BlockSpec((inner, cols), lambda z: (0, 0)), pl.BlockSpec(memory_space=pl.ANY)],
        out_specs=[half, half],
        out_shape=[shape, shape],
        cost_estimate=pl.CostEstimate(flops=2 * rows * inner * cols, bytes_accessed=2 * rows * inner, transcendentals=0),
        compiler_params=pltpu.CompilerParams(vmem_limit_bytes=16 * 1024 * 1024),
    )(slab, sketch, after)


def plane_sum(slab, sketch, after):
    kept, away = product(slab, sketch, after)
    return spread(kept + core_swap(away), PLANE).sum(axis=0)


def full_gram(own_rows):
    wide = PLANE + ("c",)
    count = lax.axis_size(wide)
    rows = gathered(own_rows, wide).reshape(-1, own_rows.shape[1])
    cols = rows.shape[1]
    unit = cols // count
    mine = lax.dynamic_slice_in_dim(rows, lax.axis_index(wide) * unit, unit, 1)
    part = lax.dot_general(
        mine,
        rows,
        (((0,), (0,)), ((), ())),
        precision=HI,
        preferred_element_type=jnp.float32,
    )
    part = gathered(part, "z").sum(axis=0)
    return gathered(part, wide).reshape(cols, cols)


def body(slab, sketch):
    moved = shifted(sketch)
    own = plane_sum(slab, sketch, sketch)
    far = plane_sum(slab, moved, own)
    plane = jnp.concatenate((own, far), axis=2)
    own_rows = spread(plane, "z").sum(axis=0)
    gram = full_gram(own_rows)
    return solve_rows(gram, own_rows, math.sqrt(ROWS))


def solution(mesh):
    fine = Mesh(mesh.devices.reshape(8, 4, 2, 2, 2), DEVICE)
    return jax.shard_map(
        body,
        mesh=fine,
        in_specs=(P(None, DEVICE), P(DEVICE, None)),
        out_specs=P(DEVICE, None),
        check_vma=False,
    )
```

```python
import functools
import math

import jax
import jax.numpy as jnp
from jax import lax
from jax.experimental import pallas as pl
from jax.experimental.pallas import tpu as pltpu
from jax.sharding import Mesh, PartitionSpec as P

ROWS = 2048
B = 128
HI = lax.Precision.HIGHEST
PLANE = ("x", "yl", "yh")
DEVICE = ("z", "x", "yl", "yh", "c")


def wide(row):
    return jnp.broadcast_to(row, (8, B))


def nt(a, b):
    return lax.dot_general(a, b, (((1,), (1,)), ((), ())), precision=HI, preferred_element_type=jnp.float32)


def eliminate(w_ref, c_ref, s):
    r0 = 8 * s
    top = w_ref[r0 : r0 + 8, :B]
    for j in range(8):
        c_ref[8 * j : 8 * j + 8, :] = wide(top[:, r0 + j : r0 + j + 1])
    schur = {(i, j): wide(c_ref[8 * j + i : 8 * j + i + 1, :]) for j in range(8) for i in range(j, 8)}
    rows = [[wide(w_ref[r0 + i : r0 + i + 1, t * B : (t + 1) * B]) for t in range(2)] for i in range(8)]
    ratio, inverse = {}, []
    for j in range(8):
        inv = 1.0 / schur[j, j]
        inverse.append(inv)
        for i in range(j + 1, 8):
            ratio[i, j] = schur[i, j] * inv
        for i in range(j + 1, 8):
            for k in range(j + 1, i + 1):
                schur[i, k] = schur[i, k] - ratio[i, j] * schur[k, j]
        for i in range(j + 1, 8):
            for t in range(2):
                rows[i][t] = rows[i][t] - ratio[i, j] * rows[j][t]
    for i in range(8):
        w_ref[r0 + i : r0 + i + 1, B:] = (rows[i][1] * lax.rsqrt(schur[i, i]))[:1]
    if s == B // 8 - 1:
        return
    g = [None] * 8
    for i in reversed(range(8)):
        g[i] = [rows[i][t] * inverse[i] for t in range(2)]
        for k in range(i + 1, 8):
            for t in range(2):
                g[i][t] = g[i][t] - ratio[k, i] * g[k][t]
    for v in range(s + 1, B // 8):
        at = slice(8 * v, 8 * v + 8)
        left, right = w_ref[at, :B], w_ref[at, B:]
        new_left, new_right = left, right
        for j in range(8):
            col = wide(left[:, r0 + j : r0 + j + 1])
            new_left = new_left - col * g[j][0]
            new_right = new_right - col * g[j][1]
        w_ref[at, :B] = new_left
        w_ref[at, B:] = new_right


def kernel(scale, gram_ref, rows_ref, out_ref, a_ref, w_ref, c_ref):
    n = gram_ref.shape[0]
    a_ref[:n] = gram_ref[...]
    a_ref[n:] = rows_ref[...]
    eye = (lax.broadcasted_iota(jnp.int32, (B, B), 0) == lax.broadcasted_iota(jnp.int32, (B, B), 1)).astype(jnp.float32)
    for k in range(n // B):
        lo, hi = k * B, (k + 1) * B
        w_ref[:, :B] = a_ref[lo:hi, lo:hi]
        w_ref[:, B:] = eye
        for s in range(B // 8):
            eliminate(w_ref, c_ref, s)
        inv = w_ref[:, B:]
        panel = nt(a_ref[hi:, lo:hi], inv)
        out_ref[:, lo:hi] = panel[n - hi :] * scale
        if hi < n:
            a_ref[hi:, hi:] = a_ref[hi:, hi:] - nt(panel, panel[: n - hi])


def solve_rows(gram, rows, scale):
    n = gram.shape[0]
    return pl.pallas_call(
        functools.partial(kernel, scale),
        out_shape=jax.ShapeDtypeStruct(rows.shape, jnp.float32),
        in_specs=[pl.BlockSpec(memory_space=pltpu.VMEM)] * 2,
        out_specs=pl.BlockSpec(memory_space=pltpu.VMEM),
        scratch_shapes=[
            pltpu.VMEM((n + 8, n), jnp.float32),
            pltpu.VMEM((B, 2 * B), jnp.float32),
            pltpu.VMEM((64, B), jnp.float32),
        ],
        compiler_params=pltpu.CompilerParams(vmem_limit_bytes=16 * 1024 * 1024),
    )(gram, rows)


def shifted(block):
    loop = ("z", "x", "yl")
    size = lax.axis_size(loop)
    return lax.ppermute(block, loop, [(i, (i + 1) % size) for i in range(size)])


def core_swap(block):
    return lax.ppermute(block, "c", [(0, 1), (1, 0)])


def spread(block, axes):
    return lax.all_to_all(block, axes, 0, 0, tiled=True)


def gathered(block, axes):
    size = lax.axis_size(axes)
    return spread(jnp.broadcast_to(block[None], (size,) + block.shape), axes)


def own_kernel(slab_ref, sketch_ref, kept_first, away_first, kept_rest, away_rest):
    width, unit, cols = kept_first.shape
    total = jnp.dot(slab_ref[...], sketch_ref[...], preferred_element_type=jnp.float32)
    pairs = total.reshape(width, 2, unit, 2 * cols)
    low = lax.axis_index("c") == 0
    kept = jnp.where(low, pairs[:, 0], pairs[:, 1])
    away = jnp.where(low, pairs[:, 1], pairs[:, 0])
    kept_first[...], kept_rest[...] = kept[:, :, :cols], kept[:, :, cols:]
    away_first[...], away_rest[...] = away[:, :, :cols], away[:, :, cols:]


def far_kernel(slab_ref, sketch_ref, kept_own, away_own, after_ref, kept_ref, away_ref):
    width, count, unit, cols = kept_ref.shape
    total = jnp.dot(slab_ref[...], sketch_ref[...], preferred_element_type=jnp.float32)
    pairs = total.reshape(width, 2, unit, (count - 1) * cols)
    low = lax.axis_index("c") == 0
    kept = jnp.where(low, pairs[:, 0], pairs[:, 1])
    away = jnp.where(low, pairs[:, 1], pairs[:, 0])
    kept_ref[:, 0], away_ref[:, 0] = kept_own[...], away_own[...]
    for i in range(1, count):
        at = slice((i - 1) * cols, i * cols)
        kept_ref[:, i], away_ref[:, i] = kept[:, :, at], away[:, :, at]


def products(slab, sketch):
    depth, width = lax.axis_size("z"), lax.axis_size(PLANE)
    rows, inner = slab.shape
    cols = sketch.shape[1]
    unit = rows // (depth * width * 2)
    matrices = [
        pl.BlockSpec((rows // depth, inner), lambda z: (z, 0)),
        pl.BlockSpec((inner, cols), lambda z: (0, 0)),
    ]
    params = pltpu.CompilerParams(vmem_limit_bytes=56 * 1024 * 1024)
    first = pl.BlockSpec((None, width, unit, B), lambda z: (z, 0, 0, 0))
    rest = pl.BlockSpec((width, None, unit, B), lambda z: (0, z, 0, 0))
    wide_rest = pl.BlockSpec((width, None, 3, unit, B), lambda z: (0, z, 0, 0, 0))

    def shape(*dims):
        return jax.ShapeDtypeStruct(dims, jnp.float32)

    def own():
        return pl.pallas_call(
            own_kernel,
            grid=(depth,),
            in_specs=matrices,
            out_specs=[first, first, rest, rest],
            out_shape=[shape(depth, width, unit, B)] * 2 + [shape(width, depth, unit, B)] * 2,
            compiler_params=params,
        )(slab, sketch)

    def far(moved, kept_rest, away_rest, after):
        return pl.pallas_call(
            far_kernel,
            grid=(depth,),
            in_specs=matrices + [rest, rest, pl.BlockSpec(memory_space=pl.ANY)],
            out_specs=[wide_rest, wide_rest],
            out_shape=[shape(width, depth, 3, unit, B)] * 2,
            compiler_params=params,
        )(slab, moved, kept_rest, away_rest, after)

    return own, far


def summed_rows(slab, sketch, moved):
    own, far = products(slab, sketch)
    kept, away, kept_rest, away_rest = own()
    first = spread(kept + core_swap(away), "z").sum(axis=0)
    kept, away = far(moved, kept_rest, away_rest, first)
    chip = kept + core_swap(away)
    width, depth, count, unit, cols = chip.shape
    chip = chip.reshape(width, depth * count, unit, cols)
    plane = spread(jnp.concatenate((chip, first[:, None]), axis=1), PLANE).sum(axis=0)
    rest = spread(plane[:-1].reshape(depth, count, unit, cols), "z").sum(axis=0)
    return jnp.concatenate((plane[-1], rest[0], rest[1], rest[2]), axis=1)


def full_gram(own_rows):
    wide = PLANE + ("c",)
    count = lax.axis_size(wide)
    rows = gathered(own_rows, wide).reshape(-1, own_rows.shape[1])
    cols = rows.shape[1]
    unit = cols // count
    mine = lax.dynamic_slice_in_dim(rows, lax.axis_index(wide) * unit, unit, 1)
    part = lax.dot_general(
        mine,
        rows,
        (((0,), (0,)), ((), ())),
        precision=HI,
        preferred_element_type=jnp.float32,
    )
    part = gathered(part, "z").sum(axis=0)
    return gathered(part, wide).reshape(cols, cols)


def body(slab, sketch):
    moved = shifted(sketch)
    own_rows = summed_rows(slab, sketch, moved)
    gram = full_gram(own_rows)
    return solve_rows(gram, own_rows, math.sqrt(ROWS))


def solution(mesh):
    fine = Mesh(mesh.devices.reshape(8, 4, 2, 2, 2), DEVICE)
    return jax.shard_map(
        body,
        mesh=fine,
        in_specs=(P(None, DEVICE), P(DEVICE, None)),
        out_specs=P(DEVICE, None),
        check_vma=False,
    )
```

```python
import functools
import math

import jax
import jax.numpy as jnp
from jax import lax
from jax.experimental import pallas as pl
from jax.experimental.pallas import tpu as pltpu
from jax.sharding import Mesh, PartitionSpec as P

ROWS = 2048
B = 128
HI = lax.Precision.HIGHEST
PLANE = ("x", "yl", "yh")
DEVICE = ("z", "x", "yl", "yh", "c")


def wide(row):
    return jnp.broadcast_to(row, (8, B))


def nt(a, b):
    return lax.dot_general(a, b, (((1,), (1,)), ((), ())), precision=HI, preferred_element_type=jnp.float32)


def eliminate(w_ref, c_ref, s):
    r0 = 8 * s
    top = w_ref[r0 : r0 + 8, :B]
    for j in range(8):
        c_ref[8 * j : 8 * j + 8, :] = wide(top[:, r0 + j : r0 + j + 1])
    schur = {(i, j): wide(c_ref[8 * j + i : 8 * j + i + 1, :]) for j in range(8) for i in range(j, 8)}
    rows = [[wide(w_ref[r0 + i : r0 + i + 1, t * B : (t + 1) * B]) for t in range(2)] for i in range(8)]
    ratio, inverse = {}, []
    for j in range(8):
        inv = 1.0 / schur[j, j]
        inverse.append(inv)
        for i in range(j + 1, 8):
            ratio[i, j] = schur[i, j] * inv
        for i in range(j + 1, 8):
            for k in range(j + 1, i + 1):
                schur[i, k] = schur[i, k] - ratio[i, j] * schur[k, j]
        for i in range(j + 1, 8):
            for t in range(2):
                rows[i][t] = rows[i][t] - ratio[i, j] * rows[j][t]
    for i in range(8):
        w_ref[r0 + i : r0 + i + 1, B:] = (rows[i][1] * lax.rsqrt(schur[i, i]))[:1]
    if s == B // 8 - 1:
        return
    g = [None] * 8
    for i in reversed(range(8)):
        g[i] = [rows[i][t] * inverse[i] for t in range(2)]
        for k in range(i + 1, 8):
            for t in range(2):
                g[i][t] = g[i][t] - ratio[k, i] * g[k][t]
    for v in range(s + 1, B // 8):
        at = slice(8 * v, 8 * v + 8)
        left, right = w_ref[at, :B], w_ref[at, B:]
        new_left, new_right = left, right
        for j in range(8):
            col = wide(left[:, r0 + j : r0 + j + 1])
            new_left = new_left - col * g[j][0]
            new_right = new_right - col * g[j][1]
        w_ref[at, :B] = new_left
        w_ref[at, B:] = new_right


def kernel(scale, gram_ref, rows_ref, out_ref, a_ref, w_ref, c_ref):
    n = rows_ref.shape[1]
    count, unit, _ = gram_ref.shape
    for q in range(count):
        top, low = q * unit, n - (q + 1) * unit
        cut = (top // B + 1) * B
        a_ref[top : top + unit, :cut] = gram_ref[q, :, :cut]
        a_ref[low : low + unit, : (low // B + 1) * B] = gram_ref[q, :, cut:]
    a_ref[n:] = rows_ref[...]
    eye = (lax.broadcasted_iota(jnp.int32, (B, B), 0) == lax.broadcasted_iota(jnp.int32, (B, B), 1)).astype(jnp.float32)
    for lo in range(0, n, B):
        hi = lo + B
        w_ref[:, :B] = a_ref[lo:hi, lo:hi]
        w_ref[:, B:] = eye
        for s in range(B // 8):
            eliminate(w_ref, c_ref, s)
        panel = nt(a_ref[hi:, lo:hi], w_ref[:, B:])
        out_ref[:, lo:hi] = panel[n - hi :] * scale
        for at in range(hi, n, B):
            a_ref[at:, at : at + B] = a_ref[at:, at : at + B] - nt(panel[at - hi :], panel[at - hi : at - hi + B])


def solve_rows(gram, rows, scale):
    n = rows.shape[1]
    return pl.pallas_call(
        functools.partial(kernel, scale),
        out_shape=jax.ShapeDtypeStruct(rows.shape, jnp.float32),
        in_specs=[pl.BlockSpec(memory_space=pltpu.VMEM)] * 2,
        out_specs=pl.BlockSpec(memory_space=pltpu.VMEM),
        scratch_shapes=[
            pltpu.VMEM((n + 8, n), jnp.float32),
            pltpu.VMEM((B, 2 * B), jnp.float32),
            pltpu.VMEM((64, B), jnp.float32),
        ],
        compiler_params=pltpu.CompilerParams(vmem_limit_bytes=16 * 1024 * 1024),
    )(gram, rows)


def shifted(block):
    loop = ("z", "x", "yl")
    size = lax.axis_size(loop)
    return lax.ppermute(block, loop, [(i, (i + 1) % size) for i in range(size)])


def core_swap(block):
    return lax.ppermute(block, "c", [(0, 1), (1, 0)])


def spread(block, axes):
    return lax.all_to_all(block, axes, 0, 0, tiled=True)


def gathered(block, axes):
    size = lax.axis_size(axes)
    return spread(jnp.broadcast_to(block[None], (size,) + block.shape), axes)


def product_kernel(slab_ref, sketch_ref, kept_ref, away_ref):
    width, unit, cols = kept_ref.shape
    total = jnp.dot(slab_ref[...], sketch_ref[...], preferred_element_type=jnp.float32)
    pairs = total.reshape(width, 2, unit, cols)
    first = lax.axis_index("c") == 0
    kept_ref[...] = jnp.where(first, pairs[:, 0], pairs[:, 1])
    away_ref[...] = jnp.where(first, pairs[:, 1], pairs[:, 0])


def product(slab, sketch):
    depth, width = lax.axis_size("z"), lax.axis_size(PLANE)
    rows, inner = slab.shape
    cols = sketch.shape[1]
    unit = rows // (depth * width * 2)
    half = pl.BlockSpec((width, None, unit, cols), lambda z: (0, z, 0, 0))
    shape = jax.ShapeDtypeStruct((width, depth, unit, cols), jnp.float32)
    return pl.pallas_call(
        product_kernel,
        grid=(depth,),
        in_specs=[pl.BlockSpec((rows // depth, inner), lambda z: (z, 0)), pl.BlockSpec((inner, cols), lambda z: (0, 0))],
        out_specs=[half, half],
        out_shape=[shape, shape],
        cost_estimate=pl.CostEstimate(flops=2 * rows * inner * cols, bytes_accessed=2 * rows * inner, transcendentals=0),
        compiler_params=pltpu.CompilerParams(vmem_limit_bytes=16 * 1024 * 1024),
    )(slab, sketch)


def chip_sum(slab, sketch):
    kept, away = product(slab, sketch)
    return kept + core_swap(away)


def lower_gram(own_rows):
    wide_axes = PLANE + ("c",)
    count = lax.axis_size(wide_axes)
    rows = gathered(own_rows, wide_axes).reshape(-1, own_rows.shape[1])
    cols = rows.shape[1]
    unit = cols // (2 * count)
    place = lax.axis_index(wide_axes)
    top = lax.dynamic_slice_in_dim(rows, place * unit, unit, 1)
    low = lax.dynamic_slice_in_dim(rows, cols - (place + 1) * unit, unit, 1)
    part = lax.dot_general(
        jnp.concatenate((top, low), axis=1),
        rows,
        (((0,), (0,)), ((), ())),
        precision=HI,
        preferred_element_type=jnp.float32,
    )
    short = jnp.concatenate((part[:unit, :B], part[unit:]), axis=1)
    long = jnp.concatenate((part[:unit, : 2 * B], part[unit:, : 3 * B]), axis=1)
    packed = jnp.where(place * unit < B, short, long)
    return gathered(gathered(packed, "z").sum(axis=0), wide_axes)


def body(slab, sketch):
    moved = shifted(sketch)
    chip = jnp.concatenate((chip_sum(slab, sketch), chip_sum(slab, moved)), axis=3)
    own_rows = spread(spread(chip, PLANE).sum(axis=0), "z").sum(axis=0)
    return solve_rows(lower_gram(own_rows), own_rows, math.sqrt(ROWS))


def solution(mesh):
    fine = Mesh(mesh.devices.reshape(8, 4, 2, 2, 2), DEVICE)
    return jax.shard_map(
        body,
        mesh=fine,
        in_specs=(P(None, DEVICE), P(DEVICE, None)),
        out_specs=P(DEVICE, None),
        check_vma=False,
    )
```

```python
import functools
import math

import jax
import jax.numpy as jnp
from jax import lax
from jax.experimental import pallas as pl
from jax.experimental.pallas import tpu as pltpu
from jax.sharding import Mesh, PartitionSpec as P

ROWS = 2048
B = 128
HI = lax.Precision.HIGHEST
PLANE = ("x", "yl", "yh")
DEVICE = ("z", "x", "yl", "yh", "c")


def wide(row):
    return jnp.broadcast_to(row, (8, B))


def nt(a, b):
    return lax.dot_general(a, b, (((1,), (1,)), ((), ())), precision=HI, preferred_element_type=jnp.float32)


def eliminate(w_ref, c_ref, s, tasks):
    r0 = 8 * s
    last = s == B // 8 - 1
    lane = lax.broadcasted_iota(jnp.int32, (8, B), 1) - r0
    here = (lane >= 0) & (lane < 8)
    unit = jnp.where(lane == lax.broadcasted_iota(jnp.int32, (8, B), 0), 1.0, 0.0)
    top = w_ref[r0 : r0 + 8, :]
    for j in range(8):
        c_ref[8 * j : 8 * j + 8, :] = wide(top[:, r0 + j : r0 + j + 1])
    c_ref[64:72, :] = jnp.where(here, unit, top)
    schur = {(i, j): wide(c_ref[8 * j + i : 8 * j + i + 1, :]) for j in range(8) for i in range(j, 8)}
    rows = [wide(c_ref[64 + i : 65 + i, :]) for i in range(8)]
    if not last:
        if tasks and tasks[0][0] == s + 1:
            tasks.pop(0)[1]()
        after = slice(r0 + 8, r0 + 16)
        near = w_ref[after, :]
        cols = [wide(near[:, r0 + j : r0 + j + 1]) for j in range(8)]
        near = jnp.where(here, 0.0, near)
    ratio, inverse = {}, []
    for j in range(8):
        inv = 1.0 / schur[j, j]
        inverse.append(inv)
        for i in range(j + 1, 8):
            ratio[i, j] = schur[i, j] * inv
        for i in range(j + 1, 8):
            for k in range(j + 1, i + 1):
                schur[i, k] = schur[i, k] - ratio[i, j] * schur[k, j]
        for i in range(j + 1, 8):
            rows[i] = rows[i] - ratio[i, j] * rows[j]
        if not last:
            for k in range(j + 1, 8):
                cols[k] = cols[k] - ratio[k, j] * cols[j]
            near = near - cols[j] * inv * rows[j]
    if not last:
        w_ref[after, :] = near
    for i in range(8):
        w_ref[r0 + i : r0 + i + 1, :] = (rows[i] * lax.rsqrt(schur[i, i]))[:1]
    while tasks and tasks[0][0] < B:
        tasks.pop(0)[1]()
    if s >= B // 8 - 2:
        return
    g = [None] * 8
    for i in reversed(range(8)):
        g[i] = rows[i] * inverse[i]
        for k in range(i + 1, 8):
            g[i] = g[i] - ratio[k, i] * g[k]

    def update(v):
        at = slice(8 * v, 8 * v + 8)
        old = w_ref[at, :]
        new = jnp.where(here, 0.0, old)
        for j in range(8):
            new = new - wide(old[:, r0 + j : r0 + j + 1]) * g[j]
        w_ref[at, :] = new

    tasks[:0] = [(v, functools.partial(update, v)) for v in range(s + 2, B // 8)]


def kernel(scale, gram_ref, rows_ref, out_ref, a_ref, w_ref, c_ref):
    n = rows_ref.shape[1]
    count, unit, _ = gram_ref.shape
    for q in range(count):
        top, low = q * unit, n - (q + 1) * unit
        cut = (top // B + 1) * B
        a_ref[top : top + unit, :cut] = gram_ref[q, :, :cut]
        a_ref[low : low + unit, : (low // B + 1) * B] = gram_ref[q, :, cut:]
    a_ref[n:] = rows_ref[...]
    lower = lax.broadcasted_iota(jnp.int32, (B, B), 0) >= lax.broadcasted_iota(jnp.int32, (B, B), 1)
    tasks = []
    for lo in range(0, n, B):
        hi = lo + B
        w = w_ref.at[lo // B % 2]
        w[...] = a_ref[lo:hi, lo:hi]
        for s in range(B // 8):
            eliminate(w, c_ref.at[s % 2], s, tasks)
        for _, task in tasks:
            task()
        tasks = []
        inv = jnp.where(lower, w[...], 0.0)
        if hi == n:
            out_ref[:, lo:hi] = nt(a_ref[hi:, lo:hi], inv) * scale
            return
        near = nt(a_ref[hi : hi + B, lo:hi], inv)
        a_ref[hi : hi + B, hi : hi + B] = a_ref[hi : hi + B, hi : hi + B] - nt(near, near)

        def rest(lo, hi, inv, near):
            far = nt(a_ref[hi + B :, lo:hi], inv)
            out_ref[:, lo:hi] = far[-8:] * scale
            a_ref[hi + B :, hi : hi + B] = a_ref[hi + B :, hi : hi + B] - nt(far, near)
            for at in range(hi + B, n, B):
                low = far[at - hi - B :]
                a_ref[at:, at : at + B] = a_ref[at:, at : at + B] - nt(low, low[:B])

        tasks.append((B, functools.partial(rest, lo, hi, inv, near)))


def solve_rows(gram, rows, scale):
    n = rows.shape[1]
    return pl.pallas_call(
        functools.partial(kernel, scale),
        out_shape=jax.ShapeDtypeStruct(rows.shape, jnp.float32),
        in_specs=[pl.BlockSpec(memory_space=pltpu.VMEM)] * 2,
        out_specs=pl.BlockSpec(memory_space=pltpu.VMEM),
        scratch_shapes=[
            pltpu.VMEM((n + 8, n), jnp.float32),
            pltpu.VMEM((2, B, B), jnp.float32),
            pltpu.VMEM((2, 72, B), jnp.float32),
        ],
        compiler_params=pltpu.CompilerParams(vmem_limit_bytes=16 * 1024 * 1024),
    )(gram, rows)


def shifted(block):
    loop = ("z", "x", "yl")
    size = lax.axis_size(loop)
    return lax.ppermute(block, loop, [(i, (i + 1) % size) for i in range(size)])


def core_swap(block):
    return lax.ppermute(block, "c", [(0, 1), (1, 0)])


def spread(block, axes):
    return lax.all_to_all(block, axes, 0, 0, tiled=True)


def gathered(block, axes):
    size = lax.axis_size(axes)
    return spread(jnp.broadcast_to(block[None], (size,) + block.shape), axes)


def product_kernel(slab_ref, sketch_ref, kept_ref, away_ref):
    width, unit, cols = kept_ref.shape
    total = jnp.dot(slab_ref[...], sketch_ref[...], preferred_element_type=jnp.float32)
    pairs = total.reshape(width, 2, unit, cols)
    first = lax.axis_index("c") == 0
    kept_ref[...] = jnp.where(first, pairs[:, 0], pairs[:, 1])
    away_ref[...] = jnp.where(first, pairs[:, 1], pairs[:, 0])


def product(slab, sketch):
    depth, width = lax.axis_size("z"), lax.axis_size(PLANE)
    rows, inner = slab.shape
    cols = sketch.shape[1]
    unit = rows // (depth * width * 2)
    half = pl.BlockSpec((width, None, unit, cols), lambda z: (0, z, 0, 0))
    shape = jax.ShapeDtypeStruct((width, depth, unit, cols), jnp.float32)
    return pl.pallas_call(
        product_kernel,
        grid=(depth,),
        in_specs=[pl.BlockSpec((rows // depth, inner), lambda z: (z, 0)), pl.BlockSpec((inner, cols), lambda z: (0, 0))],
        out_specs=[half, half],
        out_shape=[shape, shape],
        cost_estimate=pl.CostEstimate(flops=2 * rows * inner * cols, bytes_accessed=2 * rows * inner, transcendentals=0),
        compiler_params=pltpu.CompilerParams(vmem_limit_bytes=16 * 1024 * 1024),
    )(slab, sketch)


def chip_sum(slab, sketch):
    kept, away = product(slab, sketch)
    return kept + core_swap(away)


def lower_gram(own_rows):
    wide_axes = PLANE + ("c",)
    count = lax.axis_size(wide_axes)
    rows = gathered(own_rows, wide_axes).reshape(-1, own_rows.shape[1])
    cols = rows.shape[1]
    unit = cols // (2 * count)
    place = lax.axis_index(wide_axes)
    top = lax.dynamic_slice_in_dim(rows, place * unit, unit, 1)
    low = lax.dynamic_slice_in_dim(rows, cols - (place + 1) * unit, unit, 1)
    part = lax.dot_general(
        jnp.concatenate((top, low), axis=1),
        rows,
        (((0,), (0,)), ((), ())),
        precision=HI,
        preferred_element_type=jnp.float32,
    )
    short = jnp.concatenate((part[:unit, :B], part[unit:]), axis=1)
    long = jnp.concatenate((part[:unit, : 2 * B], part[unit:, : 3 * B]), axis=1)
    packed = jnp.where(place * unit < B, short, long)
    return gathered(gathered(packed, "z").sum(axis=0), wide_axes)


def body(slab, sketch):
    moved = shifted(sketch)
    chip = jnp.concatenate((chip_sum(slab, sketch), chip_sum(slab, moved)), axis=3)
    own_rows = spread(spread(chip, PLANE).sum(axis=0), "z").sum(axis=0)
    return solve_rows(lower_gram(own_rows), own_rows, math.sqrt(ROWS))


def solution(mesh):
    fine = Mesh(mesh.devices.reshape(8, 4, 2, 2, 2), DEVICE)
    return jax.shard_map(
        body,
        mesh=fine,
        in_specs=(P(None, DEVICE), P(DEVICE, None)),
        out_specs=P(DEVICE, None),
        check_vma=False,
    )
```

```python
import functools
import math

import jax
import jax.numpy as jnp
from jax import lax
from jax.experimental import pallas as pl
from jax.experimental.pallas import tpu as pltpu
from jax.sharding import Mesh, PartitionSpec as P

ROWS = 2048
B = 128
HI = lax.Precision.HIGHEST
PLANE = ("x", "yl", "yh")
DEVICE = ("z", "x", "yl", "yh", "c")


def wide(row):
    return jnp.broadcast_to(row, (8, B))


def nt(a, b):
    return lax.dot_general(a, b, (((1,), (1,)), ((), ())), precision=HI, preferred_element_type=jnp.float32)


def eliminate(w_ref, c_ref, s, tasks):
    r0 = 8 * s
    last = s == B // 8 - 1
    lane = lax.broadcasted_iota(jnp.int32, (8, B), 1) - r0
    here = (lane >= 0) & (lane < 8)
    unit = jnp.where(lane == lax.broadcasted_iota(jnp.int32, (8, B), 0), 1.0, 0.0)
    top = w_ref[r0 : r0 + 8, :]
    for j in range(8):
        c_ref[8 * j : 8 * j + 8, :] = wide(top[:, r0 + j : r0 + j + 1])
    c_ref[64:72, :] = jnp.where(here, unit, top)
    schur = {(i, j): wide(c_ref[8 * j + i : 8 * j + i + 1, :]) for j in range(8) for i in range(j, 8)}
    rows = [wide(c_ref[64 + i : 65 + i, :]) for i in range(8)]
    if not last:
        if tasks and tasks[0][0] == s + 1:
            tasks.pop(0)[1]()
        after = slice(r0 + 8, r0 + 16)
        near = w_ref[after, :]
        cols = [wide(near[:, r0 + j : r0 + j + 1]) for j in range(8)]
        near = jnp.where(here, 0.0, near)
    ratio, inverse = {}, []
    for j in range(8):
        inv = 1.0 / schur[j, j]
        inverse.append(inv)
        for i in range(j + 1, 8):
            ratio[i, j] = schur[i, j] * inv
        for i in range(j + 1, 8):
            for k in range(j + 1, i + 1):
                schur[i, k] = schur[i, k] - ratio[i, j] * schur[k, j]
        for i in range(j + 1, 8):
            rows[i] = rows[i] - ratio[i, j] * rows[j]
        if not last:
            for k in range(j + 1, 8):
                cols[k] = cols[k] - ratio[k, j] * cols[j]
            near = near - cols[j] * inv * rows[j]
    if not last:
        w_ref[after, :] = near
    for i in range(8):
        w_ref[r0 + i : r0 + i + 1, :] = (rows[i] * lax.rsqrt(schur[i, i]))[:1]
    while tasks and tasks[0][0] < B:
        tasks.pop(0)[1]()
    if s >= B // 8 - 2:
        return
    g = [None] * 8
    for i in reversed(range(8)):
        g[i] = rows[i] * inverse[i]
        for k in range(i + 1, 8):
            g[i] = g[i] - ratio[k, i] * g[k]

    def update(v):
        at = slice(8 * v, 8 * v + 8)
        old = w_ref[at, :]
        new = jnp.where(here, 0.0, old)
        for j in range(8):
            new = new - wide(old[:, r0 + j : r0 + j + 1]) * g[j]
        w_ref[at, :] = new

    tasks[:0] = [(v, functools.partial(update, v)) for v in range(s + 2, B // 8)]


def kernel(scale, gram_ref, rows_ref, out_ref, a_ref, w_ref, c_ref):
    n = rows_ref.shape[1]
    count, unit, _ = gram_ref.shape
    for q in range(count):
        top, low = q * unit, n - (q + 1) * unit
        cut = (top // B + 1) * B
        a_ref[top : top + unit, :cut] = gram_ref[q, :, :cut]
        a_ref[low : low + unit, : (low // B + 1) * B] = gram_ref[q, :, cut:]
    a_ref[n:] = rows_ref[...]
    lower = lax.broadcasted_iota(jnp.int32, (B, B), 0) >= lax.broadcasted_iota(jnp.int32, (B, B), 1)
    tasks = []
    for lo in range(0, n, B):
        hi = lo + B
        w = w_ref.at[lo // B % 2]
        w[...] = a_ref[lo:hi, lo:hi]
        for s in range(B // 8):
            eliminate(w, c_ref.at[s % 2], s, tasks)
        for _, task in tasks:
            task()
        tasks = []
        inv = jnp.where(lower, w[...], 0.0)
        if hi == n:
            out_ref[:, lo:hi] = nt(a_ref[hi:, lo:hi], inv) * scale
            return
        near = nt(a_ref[hi : hi + B, lo:hi], inv)
        a_ref[hi : hi + B, hi : hi + B] = a_ref[hi : hi + B, hi : hi + B] - nt(near, near)

        def rest(lo, hi, inv, near):
            far = nt(a_ref[hi + B :, lo:hi], inv)
            out_ref[:, lo:hi] = far[-8:] * scale
            a_ref[hi + B :, hi : hi + B] = a_ref[hi + B :, hi : hi + B] - nt(far, near)
            for at in range(hi + B, n, B):
                low = far[at - hi - B :]
                a_ref[at:, at : at + B] = a_ref[at:, at : at + B] - nt(low, low[:B])

        tasks.append((B, functools.partial(rest, lo, hi, inv, near)))


def solve_rows(gram, rows, scale):
    n = rows.shape[1]
    return pl.pallas_call(
        functools.partial(kernel, scale),
        out_shape=jax.ShapeDtypeStruct(rows.shape, jnp.float32),
        in_specs=[pl.BlockSpec(memory_space=pltpu.VMEM)] * 2,
        out_specs=pl.BlockSpec(memory_space=pltpu.VMEM),
        scratch_shapes=[
            pltpu.VMEM((n + 8, n), jnp.float32),
            pltpu.VMEM((2, B, B), jnp.float32),
            pltpu.VMEM((2, 72, B), jnp.float32),
        ],
        compiler_params=pltpu.CompilerParams(vmem_limit_bytes=16 * 1024 * 1024),
    )(gram, rows)


def shifted(block):
    loop = ("z", "x", "yl")
    size = lax.axis_size(loop)
    return lax.ppermute(block, loop, [(i, (i + 1) % size) for i in range(size)])


def core_swap(block):
    return lax.ppermute(block, "c", [(0, 1), (1, 0)])


def spread(block, axes):
    return lax.all_to_all(block, axes, 0, 0, tiled=True)


def gathered(block, axes):
    size = lax.axis_size(axes)
    return spread(jnp.broadcast_to(block[None], (size,) + block.shape), axes)


def halves(slab_ref, sketch_ref, unit):
    total = jnp.dot(slab_ref[...], sketch_ref[...], preferred_element_type=jnp.float32)
    pairs = total.reshape(-1, 2, unit, total.shape[1])
    first = lax.axis_index("c") == 0
    return jnp.where(first, pairs[:, 0], pairs[:, 1]), jnp.where(first, pairs[:, 1], pairs[:, 0])


def product_kernel(slab_ref, sketch_ref, *out_refs):
    width, unit, _ = out_refs[0].shape
    for i, value in enumerate(halves(slab_ref, sketch_ref, unit)):
        for j in range(4):
            side, t = divmod(j, 2)
            out_refs[4 * i + j][...] = value[side * width : (side + 1) * width, :, t * B : (t + 1) * B]


def product(slab, sketch):
    rows, inner = slab.shape
    cols = sketch.shape[1]
    depth, width = lax.axis_size("z"), lax.axis_size(PLANE) // 2
    unit = rows // (depth * width * 4)
    return pl.pallas_call(
        product_kernel,
        grid=(depth,),
        in_specs=[pl.BlockSpec((rows // depth, inner), lambda z: (z, 0)), pl.BlockSpec((inner, cols), lambda z: (0, 0))],
        out_specs=[pl.BlockSpec((width, None, unit, B), lambda z: (0, z, 0, 0))] * 8,
        out_shape=[jax.ShapeDtypeStruct((width, depth, unit, B), jnp.float32)] * 8,
        cost_estimate=pl.CostEstimate(flops=2 * rows * inner * cols, bytes_accessed=2 * rows * inner, transcendentals=0),
        compiler_params=pltpu.CompilerParams(vmem_limit_bytes=16 * 1024 * 1024),
    )(slab, sketch)


def own_sum(slab, sketch):
    parts = product(slab, sketch)
    chip = [kept + core_swap(away) for kept, away in zip(parts[:4], parts[4:])]
    low = lax.axis_index("yh") == 0
    kept = jnp.stack([jnp.where(low, chip[t], chip[2 + t]) for t in range(2)])
    away = jnp.stack([jnp.where(low, chip[2 + t], chip[t]) for t in range(2)])
    return kept, lax.ppermute(away, ("yl", "yh"), [(i, 3 - i) for i in range(4)])


def combine_kernel(own_kept, own_got, *refs):
    out_ref = refs[8]
    width = out_ref.shape[0] // 2
    for j in range(4):
        side, t = divmod(j, 2)
        out_ref[side * width : (side + 1) * width, :, t] = refs[j][...] + refs[4 + j][...]
    for t in range(2):
        out_ref[t * width : (t + 1) * width, :, 2] = own_kept[t] + own_got[t]


def combined(own, kept, got):
    width, depth, unit, _ = kept[0].shape
    return pl.pallas_call(
        combine_kernel,
        in_specs=[pl.BlockSpec(memory_space=pltpu.VMEM)] * 10,
        out_specs=pl.BlockSpec(memory_space=pltpu.VMEM),
        out_shape=jax.ShapeDtypeStruct((2 * width, depth, 3, unit, B), jnp.float32),
        compiler_params=pltpu.CompilerParams(vmem_limit_bytes=16 * 1024 * 1024),
    )(*own, *kept, *got)


def scattered_sum(slab, sketch, moved):
    own = own_sum(slab, sketch)
    parts = product(slab, moved)
    plane = spread(combined(own, parts[:4], [core_swap(away) for away in parts[4:]]), PLANE)
    count, depth, _, unit, _ = plane.shape
    far = plane[:, :, :2].sum(axis=0)
    own = plane[:, :, 2].reshape(count // 2, 2, depth, unit, B).sum(axis=0)
    both = jnp.concatenate((far, own.transpose(1, 0, 2, 3)), axis=1)
    return spread(both, "z").sum(axis=0)


def assemble_kernel(parts_ref, rows_ref, own_ref):
    count, tiles, unit, _ = parts_ref.shape
    width = count // 2
    for q in range(width):
        for c in range(2):
            at = slice((2 * q + c) * unit, (2 * q + c + 1) * unit)
            for t in range(2):
                source = 2 * (t * (width // 2) + q % (width // 2)) + c
                rows_ref[at, t * B : (t + 1) * B] = parts_ref[source, 2 + q // (width // 2)]
                rows_ref[at, (2 + t) * B : (3 + t) * B] = parts_ref[2 * q + c, t]
    place = lax.axis_index(PLANE) * 2 + lax.axis_index("c")
    own_ref[...] = rows_ref[pl.ds(pl.multiple_of(place * unit, unit), unit), :]


def assembled(parts):
    count, tiles, unit, _ = parts.shape
    return pl.pallas_call(
        assemble_kernel,
        in_specs=[pl.BlockSpec(memory_space=pltpu.VMEM)],
        out_specs=[pl.BlockSpec(memory_space=pltpu.VMEM)] * 2,
        out_shape=[
            jax.ShapeDtypeStruct((count * unit, tiles * B), jnp.float32),
            jax.ShapeDtypeStruct((unit, tiles * B), jnp.float32),
        ],
        compiler_params=pltpu.CompilerParams(vmem_limit_bytes=16 * 1024 * 1024),
    )(parts)


def lower_gram(rows):
    wide_axes = PLANE + ("c",)
    count = lax.axis_size(wide_axes)
    cols = rows.shape[1]
    unit = cols // (2 * count)
    place = lax.axis_index(wide_axes)
    top = lax.dynamic_slice_in_dim(rows, place * unit, unit, 1)
    low = lax.dynamic_slice_in_dim(rows, cols - (place + 1) * unit, unit, 1)
    part = lax.dot_general(
        jnp.concatenate((top, low), axis=1),
        rows,
        (((0,), (0,)), ((), ())),
        precision=HI,
        preferred_element_type=jnp.float32,
    )
    short = jnp.concatenate((part[:unit, :B], part[unit:]), axis=1)
    long = jnp.concatenate((part[:unit, : 2 * B], part[unit:, : 3 * B]), axis=1)
    packed = jnp.where(place * unit < B, short, long)
    return gathered(gathered(packed, "z").sum(axis=0), wide_axes)


def body(slab, sketch):
    moved = shifted(sketch)
    rows, own_rows = assembled(gathered(scattered_sum(slab, sketch, moved), PLANE + ("c",)))
    return solve_rows(lower_gram(rows), own_rows, math.sqrt(ROWS))


def solution(mesh):
    fine = Mesh(mesh.devices.reshape(8, 4, 2, 2, 2), DEVICE)
    return jax.shard_map(
        body,
        mesh=fine,
        in_specs=(P(None, DEVICE), P(DEVICE, None)),
        out_specs=P(DEVICE, None),
        check_vma=False,
    )
```

```python
import functools
import math

import jax
import jax.numpy as jnp
from jax import lax
from jax.experimental import pallas as pl
from jax.experimental.pallas import tpu as pltpu
from jax.sharding import Mesh, PartitionSpec as P

ROWS = 2048
B = 128
HI = lax.Precision.HIGHEST
PLANE = ("x", "yl", "yh")
DEVICE = ("z", "x", "yl", "yh", "c")


def wide(row):
    return jnp.broadcast_to(row, (8, B))


def nt(a, b):
    return lax.dot_general(a, b, (((1,), (1,)), ((), ())), precision=HI, preferred_element_type=jnp.float32)


def eliminate(w_ref, c_ref, s, tasks):
    r0 = 8 * s
    last = s == B // 8 - 1
    lane = lax.broadcasted_iota(jnp.int32, (8, B), 1) - r0
    here = (lane >= 0) & (lane < 8)
    unit = jnp.where(lane == lax.broadcasted_iota(jnp.int32, (8, B), 0), 1.0, 0.0)
    top = w_ref[r0 : r0 + 8, :]
    for j in range(8):
        c_ref[8 * j : 8 * j + 8, :] = wide(top[:, r0 + j : r0 + j + 1])
    c_ref[64:72, :] = jnp.where(here, unit, top)
    schur = {(i, j): wide(c_ref[8 * j + i : 8 * j + i + 1, :]) for j in range(8) for i in range(j, 8)}
    rows = [wide(c_ref[64 + i : 65 + i, :]) for i in range(8)]
    if not last:
        if tasks and tasks[0][0] == s + 1:
            tasks.pop(0)[1]()
        after = slice(r0 + 8, r0 + 16)
        near = w_ref[after, :]
        cols = [wide(near[:, r0 + j : r0 + j + 1]) for j in range(8)]
        near = jnp.where(here, 0.0, near)
    ratio, inverse = {}, []
    for j in range(8):
        inv = 1.0 / schur[j, j]
        inverse.append(inv)
        for i in range(j + 1, 8):
            ratio[i, j] = schur[i, j] * inv
        for i in range(j + 1, 8):
            for k in range(j + 1, i + 1):
                schur[i, k] = schur[i, k] - ratio[i, j] * schur[k, j]
        for i in range(j + 1, 8):
            rows[i] = rows[i] - ratio[i, j] * rows[j]
        if not last:
            for k in range(j + 1, 8):
                cols[k] = cols[k] - ratio[k, j] * cols[j]
            near = near - cols[j] * inv * rows[j]
    if not last:
        w_ref[after, :] = near
    for i in range(8):
        w_ref[r0 + i : r0 + i + 1, :] = (rows[i] * lax.rsqrt(schur[i, i]))[:1]
    while tasks and tasks[0][0] < B:
        tasks.pop(0)[1]()
    if s >= B // 8 - 2:
        return
    g = [None] * 8
    for i in reversed(range(8)):
        g[i] = rows[i] * inverse[i]
        for k in range(i + 1, 8):
            g[i] = g[i] - ratio[k, i] * g[k]

    def update(v):
        at = slice(8 * v, 8 * v + 8)
        old = w_ref[at, :]
        new = jnp.where(here, 0.0, old)
        for j in range(8):
            new = new - wide(old[:, r0 + j : r0 + j + 1]) * g[j]
        w_ref[at, :] = new

    tasks[:0] = [(v, functools.partial(update, v)) for v in range(s + 2, B // 8)]


def kernel(scale, gram_ref, rows_ref, out_ref, a_ref, w_ref, c_ref):
    n = rows_ref.shape[1]
    count, unit, _ = gram_ref.shape
    for q in range(count):
        top, low = q * unit, n - (q + 1) * unit
        cut = (top // B + 1) * B
        a_ref[top : top + unit, :cut] = gram_ref[q, :, :cut]
        a_ref[low : low + unit, : (low // B + 1) * B] = gram_ref[q, :, cut:]
    a_ref[n:] = rows_ref[...]
    lower = lax.broadcasted_iota(jnp.int32, (B, B), 0) >= lax.broadcasted_iota(jnp.int32, (B, B), 1)
    tasks = []
    for lo in range(0, n, B):
        hi = lo + B
        w = w_ref.at[lo // B % 2]
        w[...] = a_ref[lo:hi, lo:hi]
        for s in range(B // 8):
            eliminate(w, c_ref.at[s % 2], s, tasks)
        for _, task in tasks:
            task()
        tasks = []
        inv = jnp.where(lower, w[...], 0.0)
        if hi == n:
            out_ref[:, lo:hi] = nt(a_ref[hi:, lo:hi], inv) * scale
            return
        near = nt(a_ref[hi : hi + B, lo:hi], inv)
        a_ref[hi : hi + B, hi : hi + B] = a_ref[hi : hi + B, hi : hi + B] - nt(near, near)

        def rest(lo, hi, inv, near):
            far = nt(a_ref[hi + B :, lo:hi], inv)
            out_ref[:, lo:hi] = far[-8:] * scale
            a_ref[hi + B :, hi : hi + B] = a_ref[hi + B :, hi : hi + B] - nt(far, near)
            for at in range(hi + B, n, B):
                low = far[at - hi - B :]
                a_ref[at:, at : at + B] = a_ref[at:, at : at + B] - nt(low, low[:B])

        tasks.append((B, functools.partial(rest, lo, hi, inv, near)))


def solve_rows(gram, rows, scale):
    n = rows.shape[1]
    return pl.pallas_call(
        functools.partial(kernel, scale),
        out_shape=jax.ShapeDtypeStruct(rows.shape, jnp.float32),
        in_specs=[pl.BlockSpec(memory_space=pltpu.VMEM)] * 2,
        out_specs=pl.BlockSpec(memory_space=pltpu.VMEM),
        scratch_shapes=[
            pltpu.VMEM((n + 8, n), jnp.float32),
            pltpu.VMEM((2, B, B), jnp.float32),
            pltpu.VMEM((2, 72, B), jnp.float32),
        ],
        compiler_params=pltpu.CompilerParams(vmem_limit_bytes=16 * 1024 * 1024),
    )(gram, rows)


def shifted(block):
    loop = ("z", "x", "yl")
    size = lax.axis_size(loop)
    return lax.ppermute(block, loop, [(i, (i + 1) % size) for i in range(size)])


def core_swap(block):
    return lax.ppermute(block, "c", [(0, 1), (1, 0)])


def spread(block, axes):
    return lax.all_to_all(block, axes, 0, 0, tiled=True)


def gathered(block, axes):
    size = lax.axis_size(axes)
    return spread(jnp.broadcast_to(block[None], (size,) + block.shape), axes)


def store_halves(z, slab_ref, sketch_ref, out_refs):
    width, depth, unit, _ = out_refs[0].shape
    step = slab_ref.shape[0] // depth
    block = slab_ref[pl.ds(pl.multiple_of(z * step, step), step), :]
    total = jnp.dot(block, sketch_ref[...], preferred_element_type=jnp.float32)
    pairs = total.reshape(2 * width, 2, unit, total.shape[1])
    first = lax.axis_index("c") == 0
    values = jnp.where(first, pairs[:, 0], pairs[:, 1]), jnp.where(first, pairs[:, 1], pairs[:, 0])
    for i, value in enumerate(values):
        for j in range(4):
            side, t = divmod(j, 2)
            out_refs[4 * i + j][:, z] = value[side * width : (side + 1) * width, :, t * B : (t + 1) * B]


def own_kernel(slab_ref, sketch_ref, local_ref, *refs):
    out_refs, sems = refs[:8], refs[8]
    depth = out_refs[0].shape[1]
    step = slab_ref.shape[0] // depth

    def fetch(z):
        rows = pl.ds(pl.multiple_of(z * step, step), step)
        return pltpu.make_async_copy(slab_ref.at[rows, :], local_ref.at[rows, :], sems.at[z])

    for z in range(depth):
        fetch(z).start()

    @pl.loop(0, depth)
    def _(z):
        fetch(z).wait()
        store_halves(z, local_ref, sketch_ref, out_refs)


def far_kernel(slab_ref, sketch_ref, *out_refs):
    @pl.loop(0, out_refs[0].shape[1])
    def _(z):
        store_halves(z, slab_ref, sketch_ref, out_refs)


def product(slab, sketch, fetched):
    rows, inner = slab.shape
    cols = sketch.shape[1]
    depth, width = lax.axis_size("z"), lax.axis_size(PLANE) // 2
    unit = rows // (depth * width * 4)
    vmem = pl.BlockSpec(memory_space=pltpu.VMEM)
    parts = [jax.ShapeDtypeStruct((width, depth, unit, B), jnp.float32)] * 8
    local = [] if fetched else [jax.ShapeDtypeStruct(slab.shape, slab.dtype)]
    return pl.pallas_call(
        far_kernel if fetched else own_kernel,
        in_specs=[vmem if fetched else pl.BlockSpec(memory_space=pl.ANY), vmem],
        out_specs=[vmem] * len(local + parts),
        out_shape=local + parts,
        scratch_shapes=[] if fetched else [pltpu.SemaphoreType.DMA((depth,))],
        cost_estimate=pl.CostEstimate(flops=2 * rows * inner * cols, bytes_accessed=2 * rows * inner, transcendentals=0),
        compiler_params=pltpu.CompilerParams(vmem_limit_bytes=24 * 1024 * 1024),
    )(slab, sketch)


def own_sum(slab, sketch):
    local, *parts = product(slab, sketch, False)
    chip = [kept + core_swap(away) for kept, away in zip(parts[:4], parts[4:])]
    low = lax.axis_index("yh") == 0
    kept = jnp.stack([jnp.where(low, chip[t], chip[2 + t]) for t in range(2)])
    away = jnp.stack([jnp.where(low, chip[2 + t], chip[t]) for t in range(2)])
    got = lax.ppermute(away, ("yl", "yh"), [(i, 3 - i) for i in range(4)])
    return local, (kept, got)


def combine_kernel(own_kept, own_got, *refs):
    out_ref = refs[8]
    width = out_ref.shape[0] // 2
    for j in range(4):
        side, t = divmod(j, 2)
        out_ref[side * width : (side + 1) * width, :, t] = refs[j][...] + refs[4 + j][...]
    for t in range(2):
        out_ref[t * width : (t + 1) * width, :, 2] = own_kept[t] + own_got[t]


def combined(own, kept, got):
    width, depth, unit, _ = kept[0].shape
    return pl.pallas_call(
        combine_kernel,
        in_specs=[pl.BlockSpec(memory_space=pltpu.VMEM)] * 10,
        out_specs=pl.BlockSpec(memory_space=pltpu.VMEM),
        out_shape=jax.ShapeDtypeStruct((2 * width, depth, 3, unit, B), jnp.float32),
        compiler_params=pltpu.CompilerParams(vmem_limit_bytes=16 * 1024 * 1024),
    )(*own, *kept, *got)


def scattered_sum(slab, sketch, moved):
    local, own = own_sum(slab, sketch)
    parts = product(local, moved, True)
    plane = spread(combined(own, parts[:4], [core_swap(away) for away in parts[4:]]), PLANE)
    count, depth, _, unit, _ = plane.shape
    far = plane[:, :, :2].sum(axis=0)
    own = plane[:, :, 2].reshape(count // 2, 2, depth, unit, B).sum(axis=0)
    both = jnp.concatenate((far, own.transpose(1, 0, 2, 3)), axis=1)
    return spread(both, "z").sum(axis=0)


def assemble_kernel(parts_ref, rows_ref, own_ref):
    count, tiles, unit, _ = parts_ref.shape
    width = count // 2
    for q in range(width):
        for c in range(2):
            at = slice((2 * q + c) * unit, (2 * q + c + 1) * unit)
            for t in range(2):
                source = 2 * (t * (width // 2) + q % (width // 2)) + c
                rows_ref[at, t * B : (t + 1) * B] = parts_ref[source, 2 + q // (width // 2)]
                rows_ref[at, (2 + t) * B : (3 + t) * B] = parts_ref[2 * q + c, t]
    place = lax.axis_index(PLANE) * 2 + lax.axis_index("c")
    own_ref[...] = rows_ref[pl.ds(pl.multiple_of(place * unit, unit), unit), :]


def assembled(parts):
    count, tiles, unit, _ = parts.shape
    return pl.pallas_call(
        assemble_kernel,
        in_specs=[pl.BlockSpec(memory_space=pltpu.VMEM)],
        out_specs=[pl.BlockSpec(memory_space=pltpu.VMEM)] * 2,
        out_shape=[
            jax.ShapeDtypeStruct((count * unit, tiles * B), jnp.float32),
            jax.ShapeDtypeStruct((unit, tiles * B), jnp.float32),
        ],
        compiler_params=pltpu.CompilerParams(vmem_limit_bytes=16 * 1024 * 1024),
    )(parts)


def lower_gram(rows):
    wide_axes = PLANE + ("c",)
    count = lax.axis_size(wide_axes)
    cols = rows.shape[1]
    unit = cols // (2 * count)
    place = lax.axis_index(wide_axes)
    top = lax.dynamic_slice_in_dim(rows, place * unit, unit, 1)
    low = lax.dynamic_slice_in_dim(rows, cols - (place + 1) * unit, unit, 1)
    part = lax.dot_general(
        jnp.concatenate((top, low), axis=1),
        rows,
        (((0,), (0,)), ((), ())),
        precision=HI,
        preferred_element_type=jnp.float32,
    )
    short = jnp.concatenate((part[:unit, :B], part[unit:]), axis=1)
    long = jnp.concatenate((part[:unit, : 2 * B], part[unit:, : 3 * B]), axis=1)
    packed = jnp.where(place * unit < B, short, long)
    return gathered(gathered(packed, "z").sum(axis=0), wide_axes)


def body(slab, sketch):
    moved = shifted(sketch)
    rows, own_rows = assembled(gathered(scattered_sum(slab, sketch, moved), PLANE + ("c",)))
    return solve_rows(lower_gram(rows), own_rows, math.sqrt(ROWS))


def solution(mesh):
    fine = Mesh(mesh.devices.reshape(8, 4, 2, 2, 2), DEVICE)
    return jax.shard_map(
        body,
        mesh=fine,
        in_specs=(P(None, DEVICE), P(DEVICE, None)),
        out_specs=P(DEVICE, None),
        check_vma=False,
    )
```

```python
import functools
import math

import jax
import jax.numpy as jnp
from jax import lax
from jax.experimental import pallas as pl
from jax.experimental.pallas import tpu as pltpu
from jax.sharding import Mesh, PartitionSpec as P

ROWS = 2048
B = 128
HI = lax.Precision.HIGHEST
PLANE = ("x", "yl", "yh")
DEVICE = ("z", "x", "yl", "yh", "c")


def wide(row):
    return jnp.broadcast_to(row, (8, B))


def nt(a, b):
    return lax.dot_general(a, b, (((1,), (1,)), ((), ())), precision=HI, preferred_element_type=jnp.float32)


def eliminate(w_ref, c_ref, s, tasks):
    r0 = 8 * s
    last = s == B // 8 - 1
    lane = lax.broadcasted_iota(jnp.int32, (8, B), 1) - r0
    here = (lane >= 0) & (lane < 8)
    unit = jnp.where(lane == lax.broadcasted_iota(jnp.int32, (8, B), 0), 1.0, 0.0)
    top = w_ref[r0 : r0 + 8, :]
    for j in range(8):
        c_ref[8 * j : 8 * j + 8, :] = wide(top[:, r0 + j : r0 + j + 1])
    c_ref[64:72, :] = jnp.where(here, unit, top)
    schur = {(i, j): wide(c_ref[8 * j + i : 8 * j + i + 1, :]) for j in range(8) for i in range(j, 8)}
    rows = [wide(c_ref[64 + i : 65 + i, :]) for i in range(8)]
    if not last:
        if tasks and tasks[0][0] == s + 1:
            tasks.pop(0)[1]()
        after = slice(r0 + 8, r0 + 16)
        near = w_ref[after, :]
        cols = [wide(near[:, r0 + j : r0 + j + 1]) for j in range(8)]
        near = jnp.where(here, 0.0, near)
    ratio, inverse = {}, []
    for j in range(8):
        inv = 1.0 / schur[j, j]
        inverse.append(inv)
        for i in range(j + 1, 8):
            ratio[i, j] = schur[i, j] * inv
        for i in range(j + 1, 8):
            for k in range(j + 1, i + 1):
                schur[i, k] = schur[i, k] - ratio[i, j] * schur[k, j]
        for i in range(j + 1, 8):
            rows[i] = rows[i] - ratio[i, j] * rows[j]
        if not last:
            for k in range(j + 1, 8):
                cols[k] = cols[k] - ratio[k, j] * cols[j]
            near = near - cols[j] * inv * rows[j]
    if not last:
        w_ref[after, :] = near
    for i in range(8):
        w_ref[r0 + i : r0 + i + 1, :] = (rows[i] * lax.rsqrt(schur[i, i]))[:1]
    while tasks and tasks[0][0] < B:
        tasks.pop(0)[1]()
    if s >= B // 8 - 2:
        return
    g = [None] * 8
    for i in reversed(range(8)):
        g[i] = rows[i] * inverse[i]
        for k in range(i + 1, 8):
            g[i] = g[i] - ratio[k, i] * g[k]

    def update(v):
        at = slice(8 * v, 8 * v + 8)
        old = w_ref[at, :]
        new = jnp.where(here, 0.0, old)
        for j in range(8):
            new = new - wide(old[:, r0 + j : r0 + j + 1]) * g[j]
        w_ref[at, :] = new

    tasks[:0] = [(v, functools.partial(update, v)) for v in range(s + 2, B // 8)]


def kernel(scale, gram_ref, rows_ref, out_ref, a_ref, w_ref, c_ref):
    n = rows_ref.shape[1]
    count, unit, _ = gram_ref.shape
    for q in range(count):
        top, low = q * unit, n - (q + 1) * unit
        cut = (top // B + 1) * B
        a_ref[top : top + unit, :cut] = gram_ref[q, :, :cut]
        a_ref[low : low + unit, : (low // B + 1) * B] = gram_ref[q, :, cut:]
    a_ref[n:] = rows_ref[...]
    lower = lax.broadcasted_iota(jnp.int32, (B, B), 0) >= lax.broadcasted_iota(jnp.int32, (B, B), 1)
    tasks = []
    for lo in range(0, n, B):
        hi = lo + B
        w = w_ref.at[lo // B % 2]
        w[...] = a_ref[lo:hi, lo:hi]
        for s in range(B // 8):
            eliminate(w, c_ref.at[s % 2], s, tasks)
        for _, task in tasks:
            task()
        tasks = []
        inv = jnp.where(lower, w[...], 0.0)
        if hi == n:
            out_ref[:, lo:hi] = nt(a_ref[hi:, lo:hi], inv) * scale
            return
        near = nt(a_ref[hi : hi + B, lo:hi], inv)
        a_ref[hi : hi + B, hi : hi + B] = a_ref[hi : hi + B, hi : hi + B] - nt(near, near)

        def rest(lo, hi, inv, near):
            far = nt(a_ref[hi + B :, lo:hi], inv)
            out_ref[:, lo:hi] = far[-8:] * scale
            a_ref[hi + B :, hi : hi + B] = a_ref[hi + B :, hi : hi + B] - nt(far, near)
            for at in range(hi + B, n, B):
                low = far[at - hi - B :]
                a_ref[at:, at : at + B] = a_ref[at:, at : at + B] - nt(low, low[:B])

        tasks.append((B, functools.partial(rest, lo, hi, inv, near)))


def solve_rows(gram, rows, scale):
    n = rows.shape[1]
    return pl.pallas_call(
        functools.partial(kernel, scale),
        out_shape=jax.ShapeDtypeStruct(rows.shape, jnp.float32),
        in_specs=[pl.BlockSpec(memory_space=pltpu.VMEM)] * 2,
        out_specs=pl.BlockSpec(memory_space=pltpu.VMEM),
        scratch_shapes=[
            pltpu.VMEM((n + 8, n), jnp.float32),
            pltpu.VMEM((2, B, B), jnp.float32),
            pltpu.VMEM((2, 72, B), jnp.float32),
        ],
        compiler_params=pltpu.CompilerParams(vmem_limit_bytes=16 * 1024 * 1024),
    )(gram, rows)


def shifted(block):
    loop = ("z", "x", "yl")
    size = lax.axis_size(loop)
    return lax.ppermute(block, loop, [(i, (i + 1) % size) for i in range(size)])


def core_swap(block):
    return lax.ppermute(block, "c", [(0, 1), (1, 0)])


def spread(block, axes):
    return lax.all_to_all(block, axes, 0, 0, tiled=True)


def gathered(block, axes):
    size = lax.axis_size(axes)
    return spread(jnp.broadcast_to(block[None], (size,) + block.shape), axes)


def store_halves(z, slab_ref, sketch_ref, out_refs):
    width, depth, unit, _ = out_refs[0].shape
    step = slab_ref.shape[0] // depth
    block = slab_ref[pl.ds(pl.multiple_of(z * step, step), step), :]
    total = jnp.dot(block, sketch_ref[...], preferred_element_type=jnp.float32)
    pairs = total.reshape(2 * width, 2, unit, total.shape[1])
    first = lax.axis_index("c") == 0
    values = jnp.where(first, pairs[:, 0], pairs[:, 1]), jnp.where(first, pairs[:, 1], pairs[:, 0])
    for i, value in enumerate(values):
        for j in range(4):
            side, t = divmod(j, 2)
            out_refs[4 * i + j][:, z] = value[side * width : (side + 1) * width, :, t * B : (t + 1) * B]


def own_kernel(slab_ref, sketch_ref, local_ref, *refs):
    out_refs, sems = refs[:8], refs[8]
    depth = out_refs[0].shape[1]
    step = slab_ref.shape[0] // depth

    def fetch(z):
        rows = pl.ds(pl.multiple_of(z * step, step), step)
        return pltpu.make_async_copy(slab_ref.at[rows, :], local_ref.at[rows, :], sems.at[z])

    for z in range(depth):
        fetch(z).start()

    @pl.loop(0, depth)
    def _(z):
        fetch(z).wait()
        store_halves(z, local_ref, sketch_ref, out_refs)


def far_kernel(slab_ref, sketch_ref, *out_refs):
    @pl.loop(0, out_refs[0].shape[1])
    def _(z):
        store_halves(z, slab_ref, sketch_ref, out_refs)


def product(slab, sketch, fetched):
    rows, inner = slab.shape
    cols = sketch.shape[1]
    depth, width = lax.axis_size("z"), lax.axis_size(PLANE) // 2
    unit = rows // (depth * width * 4)
    vmem = pl.BlockSpec(memory_space=pltpu.VMEM)
    parts = [jax.ShapeDtypeStruct((width, depth, unit, B), jnp.float32)] * 8
    local = [] if fetched else [jax.ShapeDtypeStruct(slab.shape, slab.dtype)]
    return pl.pallas_call(
        far_kernel if fetched else own_kernel,
        in_specs=[vmem if fetched else pl.BlockSpec(memory_space=pl.ANY), vmem],
        out_specs=[vmem] * len(local + parts),
        out_shape=local + parts,
        scratch_shapes=[] if fetched else [pltpu.SemaphoreType.DMA((depth,))],
        cost_estimate=pl.CostEstimate(flops=2 * rows * inner * cols, bytes_accessed=2 * rows * inner, transcendentals=0),
        compiler_params=pltpu.CompilerParams(vmem_limit_bytes=24 * 1024 * 1024),
    )(slab, sketch)


def pair_kernel(*refs):
    kept_ref, away_ref = refs[8:]
    low = lax.axis_index("yh") == 0
    for q in range(kept_ref.shape[1]):
        for t in range(2):
            first = refs[t][q] + refs[4 + t][q]
            second = refs[2 + t][q] + refs[6 + t][q]
            kept_ref[t, q] = jnp.where(low, first, second)
            away_ref[t, q] = jnp.where(low, second, first)


def own_sum(slab, sketch):
    local, *parts = product(slab, sketch, False)
    vmem = pl.BlockSpec(memory_space=pltpu.VMEM)
    kept, away = pl.pallas_call(
        pair_kernel,
        in_specs=[vmem] * 8,
        out_specs=[vmem] * 2,
        out_shape=[jax.ShapeDtypeStruct((2,) + parts[0].shape, jnp.float32)] * 2,
        compiler_params=pltpu.CompilerParams(vmem_limit_bytes=16 * 1024 * 1024),
    )(*parts[:4], *[core_swap(part) for part in parts[4:]])
    got = lax.ppermute(away, ("yl", "yh"), [(i, 3 - i) for i in range(4)])
    return local, (kept, got)


def combine_kernel(own_kept, own_got, *refs):
    out_ref = refs[8]
    width = out_ref.shape[0] // 2
    for j in range(4):
        side, t = divmod(j, 2)
        out_ref[side * width : (side + 1) * width, :, t] = refs[j][...] + refs[4 + j][...]
    for t in range(2):
        out_ref[t * width : (t + 1) * width, :, 2] = own_kept[t] + own_got[t]


def combined(own, kept, got):
    width, depth, unit, _ = kept[0].shape
    return pl.pallas_call(
        combine_kernel,
        in_specs=[pl.BlockSpec(memory_space=pltpu.VMEM)] * 10,
        out_specs=pl.BlockSpec(memory_space=pltpu.VMEM),
        out_shape=jax.ShapeDtypeStruct((2 * width, depth, 3, unit, B), jnp.float32),
        compiler_params=pltpu.CompilerParams(vmem_limit_bytes=16 * 1024 * 1024),
    )(*own, *kept, *got)


def scattered_sum(slab, sketch, moved):
    local, own = own_sum(slab, sketch)
    parts = product(local, moved, True)
    plane = spread(combined(own, parts[:4], [core_swap(away) for away in parts[4:]]), PLANE)
    count, depth, _, unit, _ = plane.shape
    far = plane[:, :, :2].sum(axis=0)
    own = plane[:, :, 2].reshape(count // 2, 2, depth, unit, B).sum(axis=0)
    both = jnp.concatenate((far, own.transpose(1, 0, 2, 3)), axis=1)
    return spread(both, "z").sum(axis=0)


def assemble_kernel(parts_ref, rows_ref, own_ref):
    count, tiles, unit, _ = parts_ref.shape
    width = count // 2
    for q in range(width):
        for c in range(2):
            at = slice((2 * q + c) * unit, (2 * q + c + 1) * unit)
            for t in range(2):
                source = 2 * (t * (width // 2) + q % (width // 2)) + c
                rows_ref[at, t * B : (t + 1) * B] = parts_ref[source, 2 + q // (width // 2)]
                rows_ref[at, (2 + t) * B : (3 + t) * B] = parts_ref[2 * q + c, t]
    place = lax.axis_index(PLANE) * 2 + lax.axis_index("c")
    own_ref[...] = rows_ref[pl.ds(pl.multiple_of(place * unit, unit), unit), :]


def assembled(parts):
    count, tiles, unit, _ = parts.shape
    return pl.pallas_call(
        assemble_kernel,
        in_specs=[pl.BlockSpec(memory_space=pltpu.VMEM)],
        out_specs=[pl.BlockSpec(memory_space=pltpu.VMEM)] * 2,
        out_shape=[
            jax.ShapeDtypeStruct((count * unit, tiles * B), jnp.float32),
            jax.ShapeDtypeStruct((unit, tiles * B), jnp.float32),
        ],
        compiler_params=pltpu.CompilerParams(vmem_limit_bytes=16 * 1024 * 1024),
    )(parts)


def lower_gram(rows):
    wide_axes = PLANE + ("c",)
    count = lax.axis_size(wide_axes)
    cols = rows.shape[1]
    unit = cols // (2 * count)
    place = lax.axis_index(wide_axes)
    top = lax.dynamic_slice_in_dim(rows, place * unit, unit, 1)
    low = lax.dynamic_slice_in_dim(rows, cols - (place + 1) * unit, unit, 1)
    part = lax.dot_general(
        jnp.concatenate((top, low), axis=1),
        rows,
        (((0,), (0,)), ((), ())),
        precision=HI,
        preferred_element_type=jnp.float32,
    )
    short = jnp.concatenate((part[:unit, :B], part[unit:]), axis=1)
    long = jnp.concatenate((part[:unit, : 2 * B], part[unit:, : 3 * B]), axis=1)
    packed = jnp.where(place * unit < B, short, long)
    return gathered(gathered(packed, "z").sum(axis=0), wide_axes)


def body(slab, sketch):
    moved = shifted(sketch)
    rows, own_rows = assembled(gathered(scattered_sum(slab, sketch, moved), PLANE + ("c",)))
    return solve_rows(lower_gram(rows), own_rows, math.sqrt(ROWS))


def solution(mesh):
    fine = Mesh(mesh.devices.reshape(8, 4, 2, 2, 2), DEVICE)
    return jax.shard_map(
        body,
        mesh=fine,
        in_specs=(P(None, DEVICE), P(DEVICE, None)),
        out_specs=P(DEVICE, None),
        check_vma=False,
    )
```

```python
import functools
import math

import jax
import jax.numpy as jnp
from jax import lax
from jax.experimental import pallas as pl
from jax.experimental.pallas import tpu as pltpu
from jax.sharding import Mesh, PartitionSpec as P

ROWS = 2048
B = 128
HI = lax.Precision.HIGHEST
PLANE = ("x", "yl", "yh")
DEVICE = ("z", "x", "yl", "yh", "c")


def wide(row):
    return jnp.broadcast_to(row, (8, B))


def nt(a, b):
    return lax.dot_general(a, b, (((1,), (1,)), ((), ())), precision=HI, preferred_element_type=jnp.float32)


def eliminate(w_ref, c_ref, s, tasks):
    r0 = 8 * s
    last = s == B // 8 - 1
    lane = lax.broadcasted_iota(jnp.int32, (8, B), 1) - r0
    here = (lane >= 0) & (lane < 8)
    unit = jnp.where(lane == lax.broadcasted_iota(jnp.int32, (8, B), 0), 1.0, 0.0)
    top = w_ref[r0 : r0 + 8, :]
    for j in range(8):
        c_ref[8 * j : 8 * j + 8, :] = wide(top[:, r0 + j : r0 + j + 1])
    c_ref[64:72, :] = jnp.where(here, unit, top)
    schur = {(i, j): wide(c_ref[8 * j + i : 8 * j + i + 1, :]) for j in range(8) for i in range(j, 8)}
    rows = [wide(c_ref[64 + i : 65 + i, :]) for i in range(8)]
    if not last:
        if tasks and tasks[0][0] == s + 1:
            tasks.pop(0)[1]()
        after = slice(r0 + 8, r0 + 16)
        near = w_ref[after, :]
        cols = [wide(near[:, r0 + j : r0 + j + 1]) for j in range(8)]
        near = jnp.where(here, 0.0, near)
    ratio, inverse = {}, []
    for j in range(8):
        inv = 1.0 / schur[j, j]
        inverse.append(inv)
        for i in range(j + 1, 8):
            ratio[i, j] = schur[i, j] * inv
        for i in range(j + 1, 8):
            for k in range(j + 1, i + 1):
                schur[i, k] = schur[i, k] - ratio[i, j] * schur[k, j]
        for i in range(j + 1, 8):
            rows[i] = rows[i] - ratio[i, j] * rows[j]
        if not last:
            for k in range(j + 1, 8):
                cols[k] = cols[k] - ratio[k, j] * cols[j]
            near = near - cols[j] * inv * rows[j]
    if not last:
        w_ref[after, :] = near
    for i in range(8):
        w_ref[r0 + i : r0 + i + 1, :] = (rows[i] * lax.rsqrt(schur[i, i]))[:1]
    while tasks and tasks[0][0] < B:
        tasks.pop(0)[1]()
    if s >= B // 8 - 2:
        return
    g = [None] * 8
    for i in reversed(range(8)):
        g[i] = rows[i] * inverse[i]
        for k in range(i + 1, 8):
            g[i] = g[i] - ratio[k, i] * g[k]

    def update(v):
        at = slice(8 * v, 8 * v + 8)
        old = w_ref[at, :]
        new = jnp.where(here, 0.0, old)
        for j in range(8):
            new = new - wide(old[:, r0 + j : r0 + j + 1]) * g[j]
        w_ref[at, :] = new

    tasks[:0] = [(v, functools.partial(update, v)) for v in range(s + 2, B // 8)]


def kernel(scale, gram_ref, rows_ref, out_ref, a_ref, w_ref, c_ref):
    n = rows_ref.shape[1]
    count, unit, _ = gram_ref.shape
    for q in range(count):
        top, low = q * unit, n - (q + 1) * unit
        cut = (top // B + 1) * B
        a_ref[top : top + unit, :cut] = gram_ref[q, :, :cut]
        a_ref[low : low + unit, : (low // B + 1) * B] = gram_ref[q, :, cut:]
    a_ref[n:] = rows_ref[...]
    lower = lax.broadcasted_iota(jnp.int32, (B, B), 0) >= lax.broadcasted_iota(jnp.int32, (B, B), 1)
    tasks = []
    for lo in range(0, n, B):
        hi = lo + B
        w = w_ref.at[lo // B % 2]
        w[...] = a_ref[lo:hi, lo:hi]
        for s in range(B // 8):
            eliminate(w, c_ref.at[s % 2], s, tasks)
        for _, task in tasks:
            task()
        tasks = []
        inv = jnp.where(lower, w[...], 0.0)
        if hi == n:
            out_ref[:, lo:hi] = nt(a_ref[hi:, lo:hi], inv) * scale
            return
        near = nt(a_ref[hi : hi + B, lo:hi], inv)
        a_ref[hi : hi + B, hi : hi + B] = a_ref[hi : hi + B, hi : hi + B] - nt(near, near)

        def rest(lo, hi, inv, near):
            far = nt(a_ref[hi + B :, lo:hi], inv)
            out_ref[:, lo:hi] = far[-8:] * scale
            a_ref[hi + B :, hi : hi + B] = a_ref[hi + B :, hi : hi + B] - nt(far, near)
            for at in range(hi + B, n, B):
                low = far[at - hi - B :]
                a_ref[at:, at : at + B] = a_ref[at:, at : at + B] - nt(low, low[:B])

        tasks.append((B, functools.partial(rest, lo, hi, inv, near)))


def solve_rows(gram, rows, scale):
    n = rows.shape[1]
    return pl.pallas_call(
        functools.partial(kernel, scale),
        out_shape=jax.ShapeDtypeStruct(rows.shape, jnp.float32),
        in_specs=[pl.BlockSpec(memory_space=pltpu.VMEM)] * 2,
        out_specs=pl.BlockSpec(memory_space=pltpu.VMEM),
        scratch_shapes=[
            pltpu.VMEM((n + 8, n), jnp.float32),
            pltpu.VMEM((2, B, B), jnp.float32),
            pltpu.VMEM((2, 72, B), jnp.float32),
        ],
        compiler_params=pltpu.CompilerParams(vmem_limit_bytes=16 * 1024 * 1024),
    )(gram, rows)


def shifted(block):
    loop = ("z", "x", "yl")
    size = lax.axis_size(loop)
    return lax.ppermute(block, loop, [(i, (i + 1) % size) for i in range(size)])


def core_swap(block):
    return lax.ppermute(block, "c", [(0, 1), (1, 0)])


def spread(block, axes):
    return lax.all_to_all(block, axes, 0, 0, tiled=True)


def gathered(block, axes):
    size = lax.axis_size(axes)
    return spread(jnp.broadcast_to(block[None], (size,) + block.shape), axes)


def store_halves(z, slab_ref, sketch_ref, out_refs):
    width, depth, unit, _ = out_refs[0].shape
    step = slab_ref.shape[0] // depth
    block = slab_ref[pl.ds(pl.multiple_of(z * step, step), step), :]
    total = jnp.dot(block, sketch_ref[...], preferred_element_type=jnp.float32)
    pairs = total.reshape(2 * width, 2, unit, total.shape[1])
    first = lax.axis_index("c") == 0
    values = jnp.where(first, pairs[:, 0], pairs[:, 1]), jnp.where(first, pairs[:, 1], pairs[:, 0])
    for i, value in enumerate(values):
        for j in range(4):
            side, t = divmod(j, 2)
            out_refs[4 * i + j][:, z] = value[side * width : (side + 1) * width, :, t * B : (t + 1) * B]


def own_kernel(slab_ref, sketch_ref, local_ref, *refs):
    out_refs, sems = refs[:8], refs[8]
    depth = out_refs[0].shape[1]
    step = slab_ref.shape[0] // depth

    def fetch(z):
        rows = pl.ds(pl.multiple_of(z * step, step), step)
        return pltpu.make_async_copy(slab_ref.at[rows, :], local_ref.at[rows, :], sems.at[z])

    for z in range(depth):
        fetch(z).start()

    @pl.loop(0, depth, unroll=True)
    def _(z):
        fetch(z).wait()
        store_halves(z, local_ref, sketch_ref, out_refs)


def far_kernel(slab_ref, sketch_ref, *out_refs):
    @pl.loop(0, out_refs[0].shape[1], unroll=True)
    def _(z):
        store_halves(z, slab_ref, sketch_ref, out_refs)


def product(slab, sketch, fetched):
    rows, inner = slab.shape
    cols = sketch.shape[1]
    depth, width = lax.axis_size("z"), lax.axis_size(PLANE) // 2
    unit = rows // (depth * width * 4)
    vmem = pl.BlockSpec(memory_space=pltpu.VMEM)
    parts = [jax.ShapeDtypeStruct((width, depth, unit, B), jnp.float32)] * 8
    local = [] if fetched else [jax.ShapeDtypeStruct(slab.shape, slab.dtype)]
    return pl.pallas_call(
        far_kernel if fetched else own_kernel,
        in_specs=[vmem if fetched else pl.BlockSpec(memory_space=pl.ANY), vmem],
        out_specs=[vmem] * len(local + parts),
        out_shape=local + parts,
        scratch_shapes=[] if fetched else [pltpu.SemaphoreType.DMA((depth,))],
        cost_estimate=pl.CostEstimate(flops=2 * rows * inner * cols, bytes_accessed=2 * rows * inner, transcendentals=0),
        compiler_params=pltpu.CompilerParams(vmem_limit_bytes=24 * 1024 * 1024),
    )(slab, sketch)


def pair_kernel(*refs):
    kept_ref, away_ref = refs[8:]
    low = lax.axis_index("yh") == 0
    for q in range(kept_ref.shape[1]):
        for t in range(2):
            first = refs[t][q] + refs[4 + t][q]
            second = refs[2 + t][q] + refs[6 + t][q]
            kept_ref[t, q] = jnp.where(low, first, second)
            away_ref[t, q] = jnp.where(low, second, first)


def own_sum(slab, sketch):
    local, *parts = product(slab, sketch, False)
    vmem = pl.BlockSpec(memory_space=pltpu.VMEM)
    kept, away = pl.pallas_call(
        pair_kernel,
        in_specs=[vmem] * 8,
        out_specs=[vmem] * 2,
        out_shape=[jax.ShapeDtypeStruct((2,) + parts[0].shape, jnp.float32)] * 2,
        compiler_params=pltpu.CompilerParams(vmem_limit_bytes=16 * 1024 * 1024),
    )(*parts[:4], *[core_swap(part) for part in parts[4:]])
    got = lax.ppermute(away, ("yl", "yh"), [(i, 3 - i) for i in range(4)])
    return local, (kept, got)


def combine_kernel(own_kept, own_got, *refs):
    out_ref = refs[8]
    width = out_ref.shape[0] // 2
    for j in range(4):
        side, t = divmod(j, 2)
        out_ref[side * width : (side + 1) * width, :, t] = refs[j][...] + refs[4 + j][...]
    for t in range(2):
        out_ref[t * width : (t + 1) * width, :, 2] = own_kept[t] + own_got[t]


def combined(own, kept, got):
    width, depth, unit, _ = kept[0].shape
    return pl.pallas_call(
        combine_kernel,
        in_specs=[pl.BlockSpec(memory_space=pltpu.VMEM)] * 10,
        out_specs=pl.BlockSpec(memory_space=pltpu.VMEM),
        out_shape=jax.ShapeDtypeStruct((2 * width, depth, 3, unit, B), jnp.float32),
        compiler_params=pltpu.CompilerParams(vmem_limit_bytes=16 * 1024 * 1024),
    )(*own, *kept, *got)


def scattered_parts(slab, sketch, moved):
    local, own = own_sum(slab, sketch)
    parts = product(local, moved, True)
    plane = spread(combined(own, parts[:4], [core_swap(away) for away in parts[4:]]), PLANE)
    count, depth, _, unit, _ = plane.shape
    far = plane[:, :, :2].sum(axis=0)
    own = plane[:, :, 2].reshape(count // 2, 2, depth, unit, B).sum(axis=0)
    both = jnp.concatenate((far, own.transpose(1, 0, 2, 3)), axis=1)
    return spread(both, "z")


def copies_kernel(parts_ref, out_ref):
    total = parts_ref[0]
    for i in range(1, parts_ref.shape[0]):
        total = total + parts_ref[i]
    for i in range(out_ref.shape[0]):
        out_ref[i] = total


def gathered_sum(parts, axes):
    return spread(
        pl.pallas_call(
            copies_kernel,
            in_specs=[pl.BlockSpec(memory_space=pltpu.VMEM)],
            out_specs=pl.BlockSpec(memory_space=pltpu.VMEM),
            out_shape=jax.ShapeDtypeStruct((lax.axis_size(axes),) + parts.shape[1:], parts.dtype),
            compiler_params=pltpu.CompilerParams(vmem_limit_bytes=16 * 1024 * 1024),
        )(parts),
        axes,
    )


def assemble_kernel(parts_ref, rows_ref, own_ref):
    count, tiles, unit, _ = parts_ref.shape
    width = count // 2
    for q in range(width):
        for c in range(2):
            at = slice((2 * q + c) * unit, (2 * q + c + 1) * unit)
            for t in range(2):
                source = 2 * (t * (width // 2) + q % (width // 2)) + c
                rows_ref[at, t * B : (t + 1) * B] = parts_ref[source, 2 + q // (width // 2)]
                rows_ref[at, (2 + t) * B : (3 + t) * B] = parts_ref[2 * q + c, t]
    place = lax.axis_index(PLANE) * 2 + lax.axis_index("c")
    own_ref[...] = rows_ref[pl.ds(pl.multiple_of(place * unit, unit), unit), :]


def assembled(parts):
    count, tiles, unit, _ = parts.shape
    return pl.pallas_call(
        assemble_kernel,
        in_specs=[pl.BlockSpec(memory_space=pltpu.VMEM)],
        out_specs=[pl.BlockSpec(memory_space=pltpu.VMEM)] * 2,
        out_shape=[
            jax.ShapeDtypeStruct((count * unit, tiles * B), jnp.float32),
            jax.ShapeDtypeStruct((unit, tiles * B), jnp.float32),
        ],
        compiler_params=pltpu.CompilerParams(vmem_limit_bytes=16 * 1024 * 1024),
    )(parts)


def lower_gram(rows):
    wide_axes = PLANE + ("c",)
    count = lax.axis_size(wide_axes)
    cols = rows.shape[1]
    unit = cols // (2 * count)
    place = lax.axis_index(wide_axes)
    top = lax.dynamic_slice_in_dim(rows, place * unit, unit, 1)
    low = lax.dynamic_slice_in_dim(rows, cols - (place + 1) * unit, unit, 1)
    part = lax.dot_general(
        jnp.concatenate((top, low), axis=1),
        rows,
        (((0,), (0,)), ((), ())),
        precision=HI,
        preferred_element_type=jnp.float32,
    )
    short = jnp.concatenate((part[:unit, :B], part[unit:]), axis=1)
    long = jnp.concatenate((part[:unit, : 2 * B], part[unit:, : 3 * B]), axis=1)
    packed = jnp.where(place * unit < B, short, long)
    return gathered_sum(gathered(packed, "z"), wide_axes)


def body(slab, sketch):
    moved = shifted(sketch)
    rows, own_rows = assembled(gathered_sum(scattered_parts(slab, sketch, moved), PLANE + ("c",)))
    return solve_rows(lower_gram(rows), own_rows, math.sqrt(ROWS))


def solution(mesh):
    fine = Mesh(mesh.devices.reshape(8, 4, 2, 2, 2), DEVICE)
    return jax.shard_map(
        body,
        mesh=fine,
        in_specs=(P(None, DEVICE), P(DEVICE, None)),
        out_specs=P(DEVICE, None),
        check_vma=False,
    )
```

```python
import functools
import math

import jax
import jax.numpy as jnp
from jax import lax
from jax.experimental import pallas as pl
from jax.experimental.pallas import tpu as pltpu
from jax.sharding import Mesh, PartitionSpec as P

ROWS = 2048
B = 128
HI = lax.Precision.HIGHEST
PLANE = ("x", "yl", "yh")
DEVICE = ("z", "x", "yl", "yh", "c")


def wide(row):
    return jnp.broadcast_to(row, (8, B))


def nt(a, b):
    return lax.dot_general(a, b, (((1,), (1,)), ((), ())), precision=HI, preferred_element_type=jnp.float32)


def eliminate(w_ref, c_ref, s, tasks):
    r0 = 8 * s
    last = s == B // 8 - 1
    lane = lax.broadcasted_iota(jnp.int32, (8, B), 1) - r0
    here = (lane >= 0) & (lane < 8)
    unit = jnp.where(lane == lax.broadcasted_iota(jnp.int32, (8, B), 0), 1.0, 0.0)
    top = w_ref[r0 : r0 + 8, :]
    for j in range(8):
        c_ref[8 * j : 8 * j + 8, :] = wide(top[:, r0 + j : r0 + j + 1])
    c_ref[64:72, :] = jnp.where(here, unit, top)
    schur = {(i, j): wide(c_ref[8 * j + i : 8 * j + i + 1, :]) for j in range(8) for i in range(j, 8)}
    rows = [wide(c_ref[64 + i : 65 + i, :]) for i in range(8)]
    if not last:
        if tasks and tasks[0][0] == s + 1:
            tasks.pop(0)[1]()
        after = slice(r0 + 8, r0 + 16)
        near = w_ref[after, :]
        cols = [wide(near[:, r0 + j : r0 + j + 1]) for j in range(8)]
        near = jnp.where(here, 0.0, near)
    ratio, inverse = {}, []
    for j in range(8):
        inv = 1.0 / schur[j, j]
        inverse.append(inv)
        for i in range(j + 1, 8):
            ratio[i, j] = schur[i, j] * inv
        for i in range(j + 1, 8):
            for k in range(j + 1, i + 1):
                schur[i, k] = schur[i, k] - ratio[i, j] * schur[k, j]
        for i in range(j + 1, 8):
            rows[i] = rows[i] - ratio[i, j] * rows[j]
        if not last:
            for k in range(j + 1, 8):
                cols[k] = cols[k] - ratio[k, j] * cols[j]
            near = near - cols[j] * inv * rows[j]
    if not last:
        w_ref[after, :] = near
    for i in range(8):
        w_ref[r0 + i : r0 + i + 1, :] = (rows[i] * lax.rsqrt(schur[i, i]))[:1]
    while tasks and tasks[0][0] < B:
        tasks.pop(0)[1]()
    if s >= B // 8 - 2:
        return
    g = [None] * 8
    for i in reversed(range(8)):
        g[i] = rows[i] * inverse[i]
        for k in range(i + 1, 8):
            g[i] = g[i] - ratio[k, i] * g[k]

    def update(v):
        at = slice(8 * v, 8 * v + 8)
        old = w_ref[at, :]
        new = jnp.where(here, 0.0, old)
        for j in range(8):
            new = new - wide(old[:, r0 + j : r0 + j + 1]) * g[j]
        w_ref[at, :] = new

    tasks[:0] = [(v, functools.partial(update, v)) for v in range(s + 2, B // 8)]


def kernel(scale, gram_ref, rows_ref, out_ref, a_ref, w_ref, c_ref):
    n = rows_ref.shape[1]
    count, unit, _ = gram_ref.shape
    for q in range(count):
        top, low = q * unit, n - (q + 1) * unit
        cut = (top // B + 1) * B
        a_ref[top : top + unit, :cut] = gram_ref[q, :, :cut]
        a_ref[low : low + unit, : (low // B + 1) * B] = gram_ref[q, :, cut:]
    a_ref[n:] = rows_ref[...]
    lower = lax.broadcasted_iota(jnp.int32, (B, B), 0) >= lax.broadcasted_iota(jnp.int32, (B, B), 1)
    tasks = []
    for lo in range(0, n, B):
        hi = lo + B
        w = w_ref.at[lo // B % 2]
        w[...] = a_ref[lo:hi, lo:hi]
        for s in range(B // 8):
            eliminate(w, c_ref.at[s % 2], s, tasks)
        for _, task in tasks:
            task()
        tasks = []
        inv = jnp.where(lower, w[...], 0.0)
        if hi == n:
            out_ref[:, lo:hi] = nt(a_ref[hi:, lo:hi], inv) * scale
            return
        near = nt(a_ref[hi : hi + B, lo:hi], inv)
        a_ref[hi : hi + B, hi : hi + B] = a_ref[hi : hi + B, hi : hi + B] - nt(near, near)

        def rest(lo, hi, inv, near):
            far = nt(a_ref[hi + B :, lo:hi], inv)
            out_ref[:, lo:hi] = far[-8:] * scale
            a_ref[hi + B :, hi : hi + B] = a_ref[hi + B :, hi : hi + B] - nt(far, near)
            for at in range(hi + B, n, B):
                low = far[at - hi - B :]
                a_ref[at:, at : at + B] = a_ref[at:, at : at + B] - nt(low, low[:B])

        tasks.append((B, functools.partial(rest, lo, hi, inv, near)))


def solve_rows(gram, rows, scale):
    n = rows.shape[1]
    return pl.pallas_call(
        functools.partial(kernel, scale),
        out_shape=jax.ShapeDtypeStruct(rows.shape, jnp.float32),
        in_specs=[pl.BlockSpec(memory_space=pltpu.VMEM)] * 2,
        out_specs=pl.BlockSpec(memory_space=pltpu.VMEM),
        scratch_shapes=[
            pltpu.VMEM((n + 8, n), jnp.float32),
            pltpu.VMEM((2, B, B), jnp.float32),
            pltpu.VMEM((2, 72, B), jnp.float32),
        ],
        compiler_params=pltpu.CompilerParams(vmem_limit_bytes=16 * 1024 * 1024),
    )(gram, rows)


def shifted(block):
    loop = ("z", "x", "yl")
    size = lax.axis_size(loop)
    return lax.ppermute(block, loop, [(i, (i + 1) % size) for i in range(size)])


def core_swap(block):
    return lax.ppermute(block, "c", [(0, 1), (1, 0)])


def spread(block, axes):
    return lax.all_to_all(block, axes, 0, 0, tiled=True)


def gathered(block, axes):
    size = lax.axis_size(axes)
    return spread(jnp.broadcast_to(block[None], (size,) + block.shape), axes)


def store_halves(z, slab_ref, sketch_ref, out_refs):
    width, depth, unit, _ = out_refs[0].shape
    step = slab_ref.shape[0] // depth
    block = slab_ref[pl.ds(pl.multiple_of(z * step, step), step), :]
    total = jnp.dot(block, sketch_ref[...], preferred_element_type=jnp.float32)
    pairs = total.reshape(2 * width, 2, unit, total.shape[1])
    first = lax.axis_index("c") == 0
    values = jnp.where(first, pairs[:, 0], pairs[:, 1]), jnp.where(first, pairs[:, 1], pairs[:, 0])
    for i, value in enumerate(values):
        for j in range(4):
            side, t = divmod(j, 2)
            out_refs[4 * i + j][:, z] = value[side * width : (side + 1) * width, :, t * B : (t + 1) * B]


def own_kernel(slab_ref, sketch_ref, local_ref, *refs):
    out_refs, sems = refs[:8], refs[8]
    depth = out_refs[0].shape[1]
    step = slab_ref.shape[0] // depth

    def fetch(z):
        rows = pl.ds(pl.multiple_of(z * step, step), step)
        return pltpu.make_async_copy(slab_ref.at[rows, :], local_ref.at[rows, :], sems.at[z])

    for z in range(depth):
        fetch(z).start()

    @pl.loop(0, depth)
    def _(z):
        fetch(z).wait()
        store_halves(z, local_ref, sketch_ref, out_refs)


def far_kernel(slab_ref, sketch_ref, *out_refs):
    @pl.loop(0, out_refs[0].shape[1], unroll=True)
    def _(z):
        store_halves(z, slab_ref, sketch_ref, out_refs)


def product(slab, sketch, fetched):
    rows, inner = slab.shape
    cols = sketch.shape[1]
    depth, width = lax.axis_size("z"), lax.axis_size(PLANE) // 2
    unit = rows // (depth * width * 4)
    vmem = pl.BlockSpec(memory_space=pltpu.VMEM)
    parts = [jax.ShapeDtypeStruct((width, depth, unit, B), jnp.float32)] * 8
    local = [] if fetched else [jax.ShapeDtypeStruct(slab.shape, slab.dtype)]
    return pl.pallas_call(
        far_kernel if fetched else own_kernel,
        in_specs=[vmem if fetched else pl.BlockSpec(memory_space=pl.ANY), vmem],
        out_specs=[vmem] * len(local + parts),
        out_shape=local + parts,
        scratch_shapes=[] if fetched else [pltpu.SemaphoreType.DMA((depth,))],
        cost_estimate=pl.CostEstimate(flops=2 * rows * inner * cols, bytes_accessed=2 * rows * inner, transcendentals=0),
        compiler_params=pltpu.CompilerParams(vmem_limit_bytes=24 * 1024 * 1024),
    )(slab, sketch)


def pair_kernel(*refs):
    kept_ref, away_ref = refs[8:]
    low = lax.axis_index("yh") == 0
    for q in range(kept_ref.shape[1]):
        for t in range(2):
            first = refs[t][q] + refs[4 + t][q]
            second = refs[2 + t][q] + refs[6 + t][q]
            kept_ref[t, q] = jnp.where(low, first, second)
            away_ref[t, q] = jnp.where(low, second, first)


def own_sum(slab, sketch):
    local, *parts = product(slab, sketch, False)
    vmem = pl.BlockSpec(memory_space=pltpu.VMEM)
    kept, away = pl.pallas_call(
        pair_kernel,
        in_specs=[vmem] * 8,
        out_specs=[vmem] * 2,
        out_shape=[jax.ShapeDtypeStruct((2,) + parts[0].shape, jnp.float32)] * 2,
        compiler_params=pltpu.CompilerParams(vmem_limit_bytes=16 * 1024 * 1024),
    )(*parts[:4], *[core_swap(part) for part in parts[4:]])
    got = lax.ppermute(away, ("yl", "yh"), [(i, 3 - i) for i in range(4)])
    return local, (kept, got)


def combine_kernel(own_kept, own_got, *refs):
    out_ref = refs[8]
    width = out_ref.shape[0] // 2
    for j in range(4):
        side, t = divmod(j, 2)
        out_ref[side * width : (side + 1) * width, :, t] = refs[j][...] + refs[4 + j][...]
    for t in range(2):
        out_ref[t * width : (t + 1) * width, :, 2] = own_kept[t] + own_got[t]


def combined(own, kept, got):
    width, depth, unit, _ = kept[0].shape
    return pl.pallas_call(
        combine_kernel,
        in_specs=[pl.BlockSpec(memory_space=pltpu.VMEM)] * 10,
        out_specs=pl.BlockSpec(memory_space=pltpu.VMEM),
        out_shape=jax.ShapeDtypeStruct((2 * width, depth, 3, unit, B), jnp.float32),
        compiler_params=pltpu.CompilerParams(vmem_limit_bytes=16 * 1024 * 1024),
    )(*own, *kept, *got)


def scattered_parts(slab, sketch, moved):
    local, own = own_sum(slab, sketch)
    parts = product(local, moved, True)
    plane = spread(combined(own, parts[:4], [core_swap(away) for away in parts[4:]]), PLANE)
    count, depth, _, unit, _ = plane.shape
    far = plane[:, :, :2].sum(axis=0)
    own = plane[:, :, 2].reshape(count // 2, 2, depth, unit, B).sum(axis=0)
    both = jnp.concatenate((far, own.transpose(1, 0, 2, 3)), axis=1)
    return spread(both, "z")


def copies_kernel(parts_ref, out_ref):
    total = parts_ref[0]
    for i in range(1, parts_ref.shape[0]):
        total = total + parts_ref[i]
    for i in range(out_ref.shape[0]):
        out_ref[i] = total


def gathered_sum(parts, axes):
    return spread(
        pl.pallas_call(
            copies_kernel,
            in_specs=[pl.BlockSpec(memory_space=pltpu.VMEM)],
            out_specs=pl.BlockSpec(memory_space=pltpu.VMEM),
            out_shape=jax.ShapeDtypeStruct((lax.axis_size(axes),) + parts.shape[1:], parts.dtype),
            compiler_params=pltpu.CompilerParams(vmem_limit_bytes=16 * 1024 * 1024),
        )(parts),
        axes,
    )


def assemble_kernel(parts_ref, rows_ref, own_ref):
    count, tiles, unit, _ = parts_ref.shape
    width = count // 2
    for q in range(width):
        for c in range(2):
            at = slice((2 * q + c) * unit, (2 * q + c + 1) * unit)
            for t in range(2):
                source = 2 * (t * (width // 2) + q % (width // 2)) + c
                rows_ref[at, t * B : (t + 1) * B] = parts_ref[source, 2 + q // (width // 2)]
                rows_ref[at, (2 + t) * B : (3 + t) * B] = parts_ref[2 * q + c, t]
    place = lax.axis_index(PLANE) * 2 + lax.axis_index("c")
    own_ref[...] = rows_ref[pl.ds(pl.multiple_of(place * unit, unit), unit), :]


def assembled(parts):
    count, tiles, unit, _ = parts.shape
    return pl.pallas_call(
        assemble_kernel,
        in_specs=[pl.BlockSpec(memory_space=pltpu.VMEM)],
        out_specs=[pl.BlockSpec(memory_space=pltpu.VMEM)] * 2,
        out_shape=[
            jax.ShapeDtypeStruct((count * unit, tiles * B), jnp.float32),
            jax.ShapeDtypeStruct((unit, tiles * B), jnp.float32),
        ],
        compiler_params=pltpu.CompilerParams(vmem_limit_bytes=16 * 1024 * 1024),
    )(parts)


def lower_gram(rows):
    wide_axes = PLANE + ("c",)
    count = lax.axis_size(wide_axes)
    cols = rows.shape[1]
    unit = cols // (2 * count)
    place = lax.axis_index(wide_axes)
    top = lax.dynamic_slice_in_dim(rows, place * unit, unit, 1)
    low = lax.dynamic_slice_in_dim(rows, cols - (place + 1) * unit, unit, 1)
    part = lax.dot_general(
        jnp.concatenate((top, low), axis=1),
        rows,
        (((0,), (0,)), ((), ())),
        precision=HI,
        preferred_element_type=jnp.float32,
    )
    short = jnp.concatenate((part[:unit, :B], part[unit:]), axis=1)
    long = jnp.concatenate((part[:unit, : 2 * B], part[unit:, : 3 * B]), axis=1)
    packed = jnp.where(place * unit < B, short, long)
    return gathered_sum(gathered(packed, "z"), wide_axes)


def body(slab, sketch):
    moved = shifted(sketch)
    rows, own_rows = assembled(gathered_sum(scattered_parts(slab, sketch, moved), PLANE + ("c",)))
    return solve_rows(lower_gram(rows), own_rows, math.sqrt(ROWS))


def solution(mesh):
    fine = Mesh(mesh.devices.reshape(8, 4, 2, 2, 2), DEVICE)
    return jax.shard_map(
        body,
        mesh=fine,
        in_specs=(P(None, DEVICE), P(DEVICE, None)),
        out_specs=P(DEVICE, None),
        check_vma=False,
    )
```
